512 devices in a mesh: dp: 32 (over x_hi, z), mp: 16 (over y, x_lo, core).
Axes of the slice: x: 4 (x_hi: 2, x_lo: 2; x = x_hi * 2 + x_lo), y: 4, z: 16, core: 2. Of those that a mesh axis runs over, the one named last changes fastest.
Arguments:
- grad_out: bfloat16 [16384, 6144], P('dp', 'mp'), may hold values from -200 to 200
- queries: bfloat16 [16384, 4096], P('dp', 'mp'), may hold values from -6.5 to 6.5
- key_rows: bfloat16 [16384, 4096], P('dp', 'mp'), may hold values from -6.5 to 6.5
- value_rows: bfloat16 [16384, 4096], P('dp', 'mp'), may hold values from -200 to 200
- out_weight: bfloat16 [4096, 6144], P('mp', 'dp'), may hold values from -0.09375 to 0.09375
- scale_exponent: int32 [], replicated, may hold values from 4 to 12
Outputs:
- grad_query: bfloat16 [16384, 4096], P('dp', 'mp')
- grad_key: bfloat16 [16384, 4096], P('dp', 'mp')
- grad_value: bfloat16 [16384, 4096], P('dp', 'mp')
- grad_weight: bfloat16 [4096, 6144], P('mp', 'dp')
- headroom: float32 [], replicated
- grad_magnitude: float32 [], replicated
The draws below stay inside these ranges and needn't reach their ends.
All inputs are finite; a program needn't handle non-finite values. Where the reference program divides by a largest or mean magnitude, that divisor is 1e-20 or more.
Results may differ from the reference program's by a relative error of at most 0.025.
Values may be sent and summed in bfloat16 or wider, within the bound.
A program may use at most 64 MiB of HBM per device.

```python
import math
from functools import partial
import jax
import jax.numpy as jnp
from jax import lax

D = 6144
H = 32
HD = 128
SEQ = 256
TOK = 512
HE = 4096
TOKENS = 16384
N_DP = 32


def column_scaling(key, columns, trend, spread_weight):
    position = jnp.arange(columns, dtype=jnp.float32) / columns
    spread = jax.random.uniform(key, (columns,), jnp.float32)
    return jnp.exp(math.log(10.0) * (trend * position + spread_weight * spread))


def row_scaling(key, rows):
    return jnp.exp(math.log(3.0) * jax.random.uniform(key, (rows, 1), jnp.float32))


def draw_queries(key, part):
    key = jax.random.fold_in(key, 11)
    return jax.random.truncated_normal(key, -6.5, 6.5, (TOKENS, H * HD), jnp.float32).astype(jnp.bfloat16)


def draw_key_rows(key, part):
    key = jax.random.fold_in(key, 12)
    return jax.random.truncated_normal(key, -6.5, 6.5, (TOKENS, H * HD), jnp.float32).astype(jnp.bfloat16)


def draw_value_rows(key, part):
    key = jax.random.fold_in(key, 13)
    first, second, third = jax.random.split(key, 3)
    columns = column_scaling(first, H * HD, 0.5, 0.5)
    base = jax.random.truncated_normal(third, -4.0, 4.0, (TOKENS, H * HD), jnp.float32)
    return (base * columns * row_scaling(second, TOKENS)).astype(jnp.bfloat16)


def draw_grad_out(key, part):
    key = jax.random.fold_in(key, 14)
    first, second, third = jax.random.split(key, 3)
    columns = column_scaling(first, D, 0.5, 0.5)
    base = jax.random.truncated_normal(third, -4.0, 4.0, (TOKENS, D), jnp.float32)
    return (base * columns * row_scaling(second, TOKENS)).astype(jnp.bfloat16)


def level_of(rng, extent, shards, low, high):
    gain = 1.0
    for axis_at, shards_of in shards:
        draws = jax.random.uniform(jax.random.fold_in(jax.random.fold_in(rng, 6), axis_at), (shards_of,), jnp.float32, low / len(shards), high / len(shards))
        gain = gain * jnp.repeat(jnp.exp(draws), extent[axis_at] // shards_of).reshape((-1,) + (1,) * (len(extent) - 1 - axis_at))
    return gain


def gaussian(own_key, extent, width, bound, cuts=(), held_as=jnp.bfloat16):
    entries = width * jax.random.normal(own_key, extent, jnp.float32)
    if cuts:
        entries = entries * level_of(own_key, extent, cuts, -0.22, 0.18)
    return jnp.clip(entries, -bound, bound).astype(held_as)


def setup_inputs(seed: int = 0) -> dict:
    keys = jax.random.split(jax.random.key(seed), 7)
    grad_out = draw_grad_out(jax.random.fold_in(keys[6], 71), 0)
    queries = draw_queries(jax.random.fold_in(keys[6], 71), 0)
    key_rows = draw_key_rows(jax.random.fold_in(keys[6], 71), 0)
    value_rows = draw_value_rows(jax.random.fold_in(keys[6], 71), 0)
    out_weight = gaussian(keys[4], (HE, D), HE ** -0.5, 0.09375, ((0, 16), (1, 32)))
    scale_exponent = jax.random.randint(keys[5], (), 4, 13).astype(jnp.int32)
    return {"grad_out": grad_out, "queries": queries, "key_rows": key_rows, "value_rows": value_rows, "out_weight": out_weight, "scale_exponent": scale_exponent}


OVERFLOW_BOUND = 65504.0
EPSILON = 1e-06

def image_backward(inverse, packed):
    queries, key_rows, value_rows, grad_context = packed
    factor = HD ** (-0.5)
    query_split = queries.astype(jnp.float32).reshape(SEQ, H, HD)
    key_split = key_rows.astype(jnp.float32).reshape(SEQ, H, HD)
    value_split = value_rows.astype(jnp.float32).reshape(SEQ, H, HD)
    grad_split = grad_context.astype(jnp.float32).reshape(SEQ, H, HD)
    scores = jnp.einsum('qhd,khd->hqk', query_split, key_split) * factor
    maxima = lax.optimization_barrier(jnp.max(scores, axis=-1, keepdims=True))
    raised = jnp.exp(scores - maxima)
    attention = raised / lax.optimization_barrier(jnp.sum(raised, axis=-1, keepdims=True))
    attention_low = lax.optimization_barrier(attention.astype(jnp.bfloat16)).astype(jnp.float32)
    context = jnp.einsum('hqk,khd->qhd', attention_low, value_split).astype(jnp.bfloat16)
    grad_value = jnp.einsum('hqk,qhd->khd', attention_low, grad_split)
    grad_attention = jnp.einsum('qhd,khd->hqk', grad_split, value_split)
    row_dots = lax.optimization_barrier(jnp.sum(attention * grad_attention, axis=-1, keepdims=True))
    grad_scores = attention * (grad_attention - row_dots) * factor
    grad_scores = lax.optimization_barrier(grad_scores.astype(jnp.bfloat16)).astype(jnp.float32)
    grad_query = jnp.einsum('hqk,khd->qhd', grad_scores, key_split)
    grad_key = jnp.einsum('hqk,qhd->khd', grad_scores, query_split)

    def finish(tensor):
        return (tensor * inverse).astype(jnp.bfloat16).reshape(SEQ, H * HD)
    return (context.reshape(SEQ, H * HD), finish(grad_query), finish(grad_key), finish(grad_value))

def reference(grad_out, queries, key_rows, value_rows, out_weight, scale_exponent):
    exponent = scale_exponent.astype(jnp.float32)
    scaling = jnp.exp2(exponent)
    inverse = jnp.exp2(-exponent)
    grad_scaled = (grad_out.astype(jnp.float32) * scaling).astype(jnp.bfloat16)
    grad_context = jnp.dot(grad_scaled, out_weight.T, preferred_element_type=jnp.float32)
    grad_context = lax.optimization_barrier(grad_context.astype(jnp.bfloat16))
    images = TOKENS // SEQ

    def regroup(matrix):
        return matrix.reshape(images, SEQ, matrix.shape[1])
    context, grad_query, grad_key, grad_value = lax.map(partial(image_backward, inverse), (regroup(queries), regroup(key_rows), regroup(value_rows), regroup(grad_context)))
    context = context.reshape(TOKENS, H * HD)
    grad_query = grad_query.reshape(TOKENS, H * HD)
    grad_key = grad_key.reshape(TOKENS, H * HD)
    grad_value = grad_value.reshape(TOKENS, H * HD)
    context_groups = context.reshape(N_DP, TOK, H * HD)
    grad_groups = grad_scaled.reshape(N_DP, TOK, D)

    def add_group(running, pair):
        block = jnp.dot(pair[0].T, pair[1], preferred_element_type=jnp.float32)
        block = lax.optimization_barrier(block.astype(jnp.bfloat16)).astype(jnp.float32)
        return (running + block, None)
    summed, _ = lax.scan(add_group, jnp.zeros((H * HD, D), jnp.float32), (context_groups, grad_groups))
    unscaled = summed * inverse
    largest = jnp.max(jnp.abs(summed))
    grad_magnitude = jnp.sqrt(jnp.sum(unscaled * unscaled) / (H * HD * D) + EPSILON)
    clipping = jnp.minimum(1.0, 1.0 / grad_magnitude)
    grad_weight = (unscaled * clipping).astype(jnp.bfloat16)
    headroom = jnp.log2(OVERFLOW_BOUND / (largest + EPSILON))
    return (grad_query, grad_key, grad_value, grad_weight, headroom, grad_magnitude)
```

```python
import jax
import jax.numpy as jnp
from jax import lax
from jax.experimental import pallas as pl
from jax.experimental.pallas import tpu as pltpu
from jax.sharding import PartitionSpec as P

D = 6144
H = 32
HD = 128
SEQ = 256
NZ = 16
NY = 4
TOK = 512
MINE = 384
HEADS = 256
COLS = 192

OVERFLOW_BOUND = 65504.0
EPSILON = 1e-06
MESH = pl.DeviceIdType.MESH
F32 = jnp.float32
BF16 = jnp.bfloat16


def dot(a, b, contract=((1,), (0,))):
    return lax.dot_general(a, b, (contract, ((), ())), preferred_element_type=F32)


def kernel(
    exponent_ref, grad_ref, q_ref, k_ref, v_ref, w_ref,
    gq_ref, gk_ref, gv_ref, gw_ref, headroom_ref, magnitude_ref,
    gf, wt, part, hop, xout, xin, att, ctx_t, acc, gc, own_sum, dp_stats, mp_stats,
    g_send, g_recv, sib_send, sib_recv, w_send, w_recv, wx_send, wx_recv,
    r_send, r_recv, x_send, x_recv, s_send, s_recv, t_send, t_recv,
):
    dp = lax.axis_index("dp")
    mp = lax.axis_index("mp")
    xh, z = dp // NZ, dp % NZ
    y, xl, c = mp // 4, (mp // 2) % 2, mp % 2
    factor = HD ** (-0.5)

    def chip(yy, xx):
        return ((yy + NY) % NY) * 2 + xx

    def to_mp(index):
        return {"dp": dp, "mp": index}

    def to_dp(index):
        return {"dp": index, "mp": mp}

    up, down = to_mp(chip(y + 1, xl) * 2 + c), to_mp(chip(y - 1, xl) * 2 + c)
    across = to_mp(chip(y, 1 - xl) * 2 + c)
    sibling = to_mp(chip(y, xl) * 2 + 1 - c)
    right, left = to_dp(xh * NZ + (z + 1) % NZ), to_dp(xh * NZ + (z + NZ - 1) % NZ)
    far = to_dp((1 - xh) * NZ + z)

    barrier = pltpu.get_barrier_semaphore()

    def greet_dp(i, _):
        pl.semaphore_signal(barrier, inc=1, device_id=to_dp((dp + i) % 32), device_id_type=MESH)
        return 0

    def greet_mp(i, _):
        pl.semaphore_signal(barrier, inc=1, device_id=to_mp((mp + i) % 16), device_id_type=MESH)
        return 0

    lax.fori_loop(1, 32, greet_dp, 0)
    lax.fori_loop(1, 16, greet_mp, 0)

    exponent = exponent_ref[0]
    scaling = lax.shift_left(jnp.int32(1), exponent).astype(F32)
    inverse = lax.shift_left(jnp.int32(1), 24 - exponent).astype(F32) * (2.0 ** -24)

    for h in range(2):
        gf[mp, h] = (grad_ref[h * SEQ : (h + 1) * SEQ, :].astype(F32) * scaling).astype(BF16)
    wt[xh, z] = w_ref[...].astype(F32).T.astype(BF16)

    pl.semaphore_wait(barrier, 46)

    def g_copy(p, h, slot, target):
        piece = gf.at[p * 2 + c, h]
        return pltpu.make_async_remote_copy(
            piece, piece, g_send.at[slot], g_recv.at[p, h], device_id=target, device_id_type=MESH
        )

    def g_wait(p, h):
        g_copy(p, h, 0, across).wait_recv()

    def sib_copy(p, cc):
        piece = gf.at[p * 2 + cc]
        return pltpu.make_async_remote_copy(
            piece, piece, sib_send.at[p], sib_recv.at[p], device_id=sibling, device_id_type=MESH
        )

    me = chip(y, xl)
    peer = chip(y, 1 - xl)
    above, below, opposite = chip(y + 1, xl), chip(y - 1, xl), chip(y + 2, xl)
    above_peer, below_peer, opposite_peer = (
        chip(y + 1, 1 - xl), chip(y - 1, 1 - xl), chip(y + 2, 1 - xl))

    def w_copy(step, direction):
        index = (z + NZ - step) % NZ if direction == 0 else (z + step) % NZ
        piece = wt.at[xh, index]
        return pltpu.make_async_remote_copy(
            piece, piece, w_send.at[direction, step], w_recv.at[direction, step],
            device_id=right if direction == 0 else left, device_id_type=MESH,
        )

    def w_arrived(step, direction):
        index = (z + NZ - step - 1) % NZ if direction == 0 else (z + step + 1) % NZ
        piece = wt.at[xh, index]
        pltpu.make_async_remote_copy(
            piece, piece, w_send.at[direction, step], w_recv.at[direction, step],
            device_id=right if direction == 0 else left, device_id_type=MESH,
        ).wait_recv()

    def w_step(step):
        for direction in range(2):
            w_arrived(step - 1, direction)
            if step < (8, 7)[direction]:
                w_copy(step, direction).start()

    def wx_copy(index, half):
        piece = wt.at[half, index]
        return pltpu.make_async_remote_copy(
            piece, piece, wx_send.at[index], wx_recv.at[index], device_id=far, device_id_type=MESH
        )

    def partial_of(m):
        block = dot(ctx_t[...], gf[m].reshape(TOK, MINE))
        turned = block.T.astype(BF16)
        part[m // 8, 2 * (m % 8)] = turned[:COLS]
        part[m // 8, 2 * (m % 8) + 1] = turned[COLS:]

    def sib_partial(p):
        sib_copy(p, 1 - c).wait_recv()
        partial_of(p * 2 + 1 - c)

    g_copy(me, 0, 0, across).start()
    g_copy(me, 0, 1, up).start()
    g_copy(me, 1, 2, down).start()
    w_copy(0, 0).start()
    w_copy(0, 1).start()
    g_copy(me, 1, 3, across).start()
    g_copy(me, 1, 4, up).start()
    g_copy(me, 0, 5, down).start()
    sib_copy(me, c).start()

    for b in range(2):
        for h in range(2):
            rows, lanes = slice(b * SEQ, (b + 1) * SEQ), slice(h * HD, (h + 1) * HD)
            scores = dot(q_ref[rows, lanes], k_ref[rows, lanes], ((1,), (1,))) * factor
            raised = jnp.exp(scores - jnp.max(scores, axis=-1, keepdims=True))
            attention = raised / jnp.sum(raised, axis=-1, keepdims=True)
            att[b * 2 + h] = attention
            context = dot(attention.astype(BF16), v_ref[rows, lanes])
            ctx_t[lanes, rows] = context.T.astype(BF16)

    w_step(1)
    g_wait(below, 0)
    g_copy(below, 0, 6, up).start()
    g_wait(above, 1)
    g_copy(above, 1, 7, down).start()
    w_step(2)
    partial_of(mp)
    g_wait(peer, 0)
    g_copy(peer, 0, 8, up).start()
    g_copy(peer, 0, 9, down).start()
    g_wait(peer, 1)
    g_copy(peer, 1, 10, up).start()
    g_copy(peer, 1, 11, down).start()
    sib_copy(peer, c).start()
    g_wait(below, 1)
    sib_copy(below, c).start()
    g_wait(above, 0)
    sib_copy(above, c).start()
    w_step(3)
    sib_partial(me)
    partial_of(peer * 2 + c)
    partial_of(below * 2 + c)
    partial_of(above * 2 + c)
    w_step(4)
    g_wait(opposite, 0)
    g_copy(opposite, 0, 12, across).start()
    g_wait(opposite, 1)
    g_copy(opposite, 1, 13, across).start()
    sib_copy(opposite, c).start()
    partial_of(opposite * 2 + c)
    w_step(5)
    sib_partial(peer)
    sib_partial(below)
    sib_partial(above)
    sib_partial(opposite)
    w_step(6)
    for p in (below_peer, above_peer, opposite_peer):
        g_wait(p, 0)
        g_wait(p, 1)
        sib_copy(p, c).start()
    for p in (below_peer, above_peer, opposite_peer):
        partial_of(p * 2 + c)
    w_step(7)
    for p in (below_peer, above_peer, opposite_peer):
        sib_partial(p)

    def r_copy(step, direction, half, source):
        return pltpu.make_async_remote_copy(
            source, hop.at[direction, step, half],
            r_send.at[direction, step, half], r_recv.at[direction, step, half],
            device_id=right if direction == 0 else left, device_id_type=MESH,
        )

    def r_dest(step, direction):
        return (z + 8 - step) % NZ if direction == 0 else (z + NZ - 7 + step) % NZ

    def r_arrived(step, direction, half):
        r_copy(step, direction, half, hop.at[direction, step, half]).wait_recv()

    def r_forward(step, direction, half):
        slot = hop.at[direction, step - 1, half]
        r_arrived(step - 1, direction, half)
        slot[...] = (
            slot[...].astype(F32) + part[half, r_dest(step, direction)].astype(F32)
        ).astype(BF16)
        r_copy(step, direction, half, slot).start()

    for half in range(2):
        for direction in range(2):
            r_copy(0, direction, half, part.at[half, r_dest(0, direction)]).start()

    w_arrived(7, 0)

    def wx_start(i, _):
        wx_copy((z + i) % NZ, xh).start()
        return 0

    lax.fori_loop(0, NZ, wx_start, 0)

    def r_step(step, _):
        for half in range(2):
            for direction in range(2):
                r_forward(step, direction, half)
        return 0

    lax.fori_loop(1, 7, r_step, 0)
    for half in range(2):
        r_forward(7, 0, half)
    for half in range(2):
        r_arrived(6, 1, half)
    for half in range(2):
        r_arrived(7, 0, half)

    def total(half):
        return (
            part[half, z].astype(F32) + hop[0, 7, half].astype(F32) + hop[1, 6, half].astype(F32)
        )

    xout[...] = total(1 - xh).astype(BF16)
    crossing = pltpu.make_async_remote_copy(
        xout, xin, x_send, x_recv, device_id=far, device_id_type=MESH
    )
    crossing.start()
    own_sum[...] = total(xh)
    crossing.wait_recv()
    summed = own_sum[...] + xin[...].astype(F32)
    own_sum[...] = summed

    unscaled = summed * inverse
    squared = unscaled * unscaled
    dp_stats[0, 0] = jnp.sum(
        (squared[:, :128] + squared[:, 128:]).reshape(COLS // 8, 8, 128), axis=0
    )
    size = jnp.abs(summed)
    dp_stats[0, 1] = jnp.max(
        jnp.maximum(size[:, :128], size[:, 128:]).reshape(COLS // 8, 8, 128), axis=0
    )

    def s_copy(i):
        return pltpu.make_async_remote_copy(
            dp_stats.at[0], dp_stats.at[i], s_send.at[i], s_recv.at[i],
            device_id=to_dp((dp + i) % 32), device_id_type=MESH,
        )

    def t_copy(i):
        return pltpu.make_async_remote_copy(
            mp_stats.at[0], mp_stats.at[i], t_send.at[i], t_recv.at[i],
            device_id=to_mp((mp + i) % 16), device_id_type=MESH,
        )

    def start(copy):
        def body(i, _):
            copy(i).start()
            return 0
        return body

    def arrive(copy):
        def body(i, _):
            copy(i).wait_recv()
            return 0
        return body

    def leave(copy):
        def body(i, _):
            copy(i).wait_send()
            return 0
        return body

    lax.fori_loop(1, 32, start(s_copy), 0)

    def wx_arrive(i, _):
        wx_copy((z + i) % NZ, 1 - xh).wait_recv()
        return 0

    lax.fori_loop(0, NZ, wx_arrive, 0)
    acc[...] = jnp.zeros_like(acc)

    def add_context(m, _):
        rows = wt[m // 8, pl.ds(2 * (m % 8), 2)].reshape(MINE, HEADS)
        acc[...] += dot(gf[m].reshape(TOK, MINE), rows)
        return 0

    lax.fori_loop(0, 16, add_context, 0)
    gc[...] = acc[...].astype(BF16)

    lax.fori_loop(1, 32, arrive(s_copy), 0)
    mp_stats[0, 0] = jnp.sum(dp_stats[:, 0], axis=0)
    mp_stats[0, 1] = jnp.max(dp_stats[:, 1], axis=0)
    lax.fori_loop(1, 16, start(t_copy), 0)

    for b in range(2):
        for h in range(2):
            rows, lanes = slice(b * SEQ, (b + 1) * SEQ), slice(h * HD, (h + 1) * HD)
            attention = att[b * 2 + h]
            grad = gc[rows, lanes]
            gv_ref[rows, lanes] = (dot(attention.T.astype(BF16), grad) * inverse).astype(BF16)
            grad_attention = dot(grad, v_ref[rows, lanes], ((1,), (1,)))
            row_dots = jnp.sum(attention * grad_attention, axis=-1, keepdims=True)
            grad_scores = attention * (grad_attention - row_dots) * factor
            gq_ref[rows, lanes] = (
                dot(grad_scores.astype(BF16), k_ref[rows, lanes]) * inverse
            ).astype(BF16)
            gk_ref[rows, lanes] = (
                dot(grad_scores.T.astype(BF16), q_ref[rows, lanes]) * inverse
            ).astype(BF16)

    lax.fori_loop(1, 16, arrive(t_copy), 0)
    squares = jnp.sum(jnp.sum(mp_stats[:, 0], axis=0), keepdims=True)
    largest = jnp.max(jnp.max(mp_stats[:, 1], axis=0), keepdims=True)
    grad_magnitude = jnp.sqrt(squares / float(H * HD * D) + EPSILON)
    clipping = jnp.minimum(1.0, 1.0 / grad_magnitude)
    gw_ref[...] = (own_sum[...] * inverse * clipping).T.astype(BF16)
    magnitude_ref[...] = jnp.broadcast_to(grad_magnitude, magnitude_ref.shape)
    headroom_ref[...] = jnp.broadcast_to(
        jnp.log2(OVERFLOW_BOUND / (largest + EPSILON)), headroom_ref.shape
    )

    for slot in range(14):
        g_copy(me, 0, slot, across).wait_send()
    for p in range(8):
        sib_copy(p, c).wait_send()
    for direction in range(2):
        for step in range((8, 7)[direction]):
            w_copy(step, direction).wait_send()
            for half in range(2):
                r_copy(step, direction, half, part.at[half, 0]).wait_send()

    def wx_leave(i, _):
        wx_copy(i, xh).wait_send()
        return 0

    lax.fori_loop(0, NZ, wx_leave, 0)
    crossing.wait_send()
    lax.fori_loop(1, 32, leave(s_copy), 0)
    lax.fori_loop(1, 16, leave(t_copy), 0)


def shards(grad_out, queries, key_rows, value_rows, out_weight, scale_exponent):
    vmem = pl.BlockSpec(memory_space=pltpu.VMEM)
    smem = pl.BlockSpec(memory_space=pltpu.SMEM)
    dma = pltpu.SemaphoreType.DMA
    outs = pl.pallas_call(
        kernel,
        out_shape=[
            jax.ShapeDtypeStruct((TOK, HEADS), BF16),
            jax.ShapeDtypeStruct((TOK, HEADS), BF16),
            jax.ShapeDtypeStruct((TOK, HEADS), BF16),
            jax.ShapeDtypeStruct((HEADS, COLS), BF16),
            jax.ShapeDtypeStruct((8, 128), F32),
            jax.ShapeDtypeStruct((8, 128), F32),
        ],
        in_specs=[smem] + [vmem] * 5,
        out_specs=[vmem] * 6,
        scratch_shapes=[
            pltpu.VMEM((16, 2, SEQ, MINE), BF16),
            pltpu.VMEM((2, NZ, COLS, HEADS), BF16),
            pltpu.VMEM((2, NZ, COLS, HEADS), BF16),
            pltpu.VMEM((2, 8, 2, COLS, HEADS), BF16),
            pltpu.VMEM((COLS, HEADS), BF16),
            pltpu.VMEM((COLS, HEADS), BF16),
            pltpu.VMEM((4, SEQ, SEQ), F32),
            pltpu.VMEM((HEADS, TOK), BF16),
            pltpu.VMEM((TOK, HEADS), F32),
            pltpu.VMEM((TOK, HEADS), BF16),
            pltpu.VMEM((COLS, HEADS), F32),
            pltpu.VMEM((32, 2, 8, 128), F32),
            pltpu.VMEM((16, 2, 8, 128), F32),
            dma((14,)), dma((8, 2)), dma((8,)), dma((8,)),
            dma((2, 8)), dma((2, 8)), dma((NZ,)), dma((NZ,)),
            dma((2, 8, 2)), dma((2, 8, 2)), dma, dma,
            dma((32,)), dma((32,)), dma((16,)), dma((16,)),
        ],
        compiler_params=pltpu.CompilerParams(
            collective_id=0, has_side_effects=True, vmem_limit_bytes=48 * 2 ** 20
        ),
    )(scale_exponent.reshape(1), grad_out, queries, key_rows, value_rows, out_weight)
    grad_query, grad_key, grad_value, grad_weight, headroom, magnitude = outs
    return (grad_query, grad_key, grad_value, grad_weight, headroom[0, 0], magnitude[0, 0])


def solution(mesh):
    placed = (P("dp", "mp"), P("dp", "mp"), P("dp", "mp"), P("dp", "mp"), P("mp", "dp"), P())
    return jax.shard_map(
        shards,
        mesh=mesh,
        in_specs=placed,
        out_specs=(P("dp", "mp"), P("dp", "mp"), P("dp", "mp"), P("mp", "dp"), P(), P()),
        check_vma=False,
    )
```

```python
import jax
import jax.numpy as jnp
from jax import lax
from jax.experimental import pallas as pl
from jax.experimental.pallas import tpu as pltpu
from jax.sharding import PartitionSpec as P

D = 6144
H = 32
HD = 128
SEQ = 256
NZ = 16
NY = 4
TOK = 512
MINE = 384
HEADS = 256
COLS = 192

OVERFLOW_BOUND = 65504.0
EPSILON = 1e-06
MESH = pl.DeviceIdType.MESH
F32 = jnp.float32
BF16 = jnp.bfloat16


def dot(a, b, contract=((1,), (0,))):
    return lax.dot_general(a, b, (contract, ((), ())), preferred_element_type=F32)


def each(first, last, body):
    def step(i, _):
        body(i)
        return 0

    lax.fori_loop(first, last, step, 0)


def remote(source, target, send, recv, device):
    return pltpu.make_async_remote_copy(
        source, target, send, recv, device_id=device, device_id_type=MESH
    )


def kernel(
    exponent_ref, grad_hbm, q_hbm, k_hbm, v_hbm, w_hbm,
    gq_ref, gk_ref, gv_ref, gw_ref, scalars_ref,
    q_ref, k_ref, v_ref, in_sem,
    gf, wt, part, hop, xout, xin, att, ctx_t, acc, gc, own_sum, stats,
    g_send, g_recv, sib_send, sib_recv, w_send, w_recv, wx_send, wx_recv,
    r_send, r_recv, x_send, x_recv, s_send, s_recv,
):
    dp = lax.axis_index("dp")
    mp = lax.axis_index("mp")
    xh, z = dp // NZ, dp % NZ
    y, xl, c = mp // 4, (mp // 2) % 2, mp % 2
    factor = HD ** (-0.5)

    near_y = y + 1 - 2 * (y % 2)
    wide_y, opposite_y = (near_y + 2) % NY, (y + 2) % NY
    me, peer = y * 2 + xl, y * 2 + 1 - xl
    near, near_peer = near_y * 2 + xl, near_y * 2 + 1 - xl
    wide, wide_peer = wide_y * 2 + xl, wide_y * 2 + 1 - xl
    opposite, opposite_peer = opposite_y * 2 + xl, opposite_y * 2 + 1 - xl

    def to_mp(index):
        return {"dp": dp, "mp": index}

    def to_dp(index):
        return {"dp": index, "mp": mp}

    to_near, to_wide = to_mp(near * 2 + c), to_mp(wide * 2 + c)
    to_peer, to_sibling = to_mp(peer * 2 + c), to_mp(me * 2 + 1 - c)
    right, left = to_dp(xh * NZ + (z + 1) % NZ), to_dp(xh * NZ + (z + NZ - 1) % NZ)
    far = to_dp((1 - xh) * NZ + z)

    barrier = pltpu.get_barrier_semaphore()
    neighbours = (to_near, to_wide, to_peer, to_sibling, right, left, far)
    for device in neighbours:
        pl.semaphore_signal(barrier, inc=1, device_id=device, device_id_type=MESH)
    loads = [
        pltpu.make_async_copy(source, target, in_sem.at[i])
        for i, (source, target) in enumerate((
            (q_hbm, q_ref), (k_hbm, k_ref), (v_hbm, v_ref),
            (grad_hbm, gf.at[mp]), (w_hbm, wt.at[xh, z]),
        ))
    ]
    for load in loads:
        load.start()

    exponent = exponent_ref[0]
    scaling = lax.shift_left(jnp.int32(1), exponent).astype(F32)
    inverse = lax.shift_left(jnp.int32(1), 24 - exponent).astype(F32) * (2.0 ** -24)

    def g_copy(p, h, slot, device):
        piece = gf.at[p * 2 + c, h]
        return remote(piece, piece, g_send.at[slot], g_recv.at[p, h], device)

    def g_own(h, slot, device):
        return remote(
            grad_hbm.at[h], gf.at[mp, h], g_send.at[slot], g_recv.at[me, h], device
        )

    def g_wait(p, h):
        g_copy(p, h, 0, to_peer).wait_recv()

    def sib_copy(p, cc):
        piece = gf.at[p * 2 + cc]
        return remote(piece, piece, sib_send.at[p], sib_recv.at[p], to_sibling)

    def w_copy(step, direction, source=None):
        piece = wt.at[xh, (z + NZ - step) % NZ if direction == 0 else (z + step) % NZ]
        return remote(
            piece if source is None else source, piece,
            w_send.at[direction, step], w_recv.at[direction, step],
            right if direction == 0 else left,
        )

    def w_arrived(step, direction):
        index = (z + NZ - step - 1) % NZ if direction == 0 else (z + step + 1) % NZ
        piece = wt.at[xh, index]
        remote(
            piece, piece, w_send.at[direction, step], w_recv.at[direction, step],
            right if direction == 0 else left,
        ).wait_recv()

    def w_step(step):
        for direction in range(2):
            if step <= (8, 7)[direction]:
                w_arrived(step - 1, direction)
            if step < (8, 7)[direction]:
                w_copy(step, direction).start()

    def wx_copy(index, half):
        piece = wt.at[half, index]
        return remote(piece, piece, wx_send.at[index], wx_recv.at[index], far)

    def wx_start(offset):
        wx_copy((z + NZ + offset) % NZ, xh).start()

    def partial_of(m):
        block = dot(ctx_t[...], gf[m].reshape(TOK, MINE))
        turned = (block.T * scaling).astype(BF16)
        part[m // 8, 2 * (m % 8)] = turned[:COLS]
        part[m // 8, 2 * (m % 8) + 1] = turned[COLS:]

    def own_partial(p):
        partial_of(p * 2 + c)

    def sib_partial(p):
        sib_copy(p, 1 - c).wait_recv()
        partial_of(p * 2 + 1 - c)

    first = y // 2

    def half_of(turn):
        return first if turn == 0 else 1 - first

    def r_copy(step, direction, turn, source):
        return remote(
            source, hop.at[direction, step, turn],
            r_send.at[direction, step, turn], r_recv.at[direction, step, turn],
            right if direction == 0 else left,
        )

    def r_dest(step, direction):
        return (z + 8 - step) % NZ if direction == 0 else (z + NZ - 7 + step) % NZ

    def r_start(turn):
        for direction in range(2):
            r_copy(0, direction, turn, part.at[half_of(turn), r_dest(0, direction)]).start()

    def r_arrived(step, direction, turn):
        r_copy(step, direction, turn, hop.at[direction, step, turn]).wait_recv()

    def r_step(step, turn):
        for direction in range(2):
            if step < (8, 7)[direction]:
                slot = hop.at[direction, step - 1, turn]
                r_arrived(step - 1, direction, turn)
                slot[...] = (
                    slot[...].astype(F32)
                    + part[half_of(turn), r_dest(step, direction)].astype(F32)
                ).astype(BF16)
                r_copy(step, direction, turn, slot).start()

    def total(turn):
        return (
            part[half_of(turn), z].astype(F32)
            + hop[0, 7, turn].astype(F32) + hop[1, 6, turn].astype(F32)
        )

    crossing = remote(xout, xin, x_send, x_recv, far)

    def finish(turn):
        r_arrived(6, 1, turn)
        r_arrived(7, 0, turn)

        @pl.when(xh == half_of(turn))
        def _():
            own_sum[...] = total(turn)

        @pl.when(xh != half_of(turn))
        def _():
            xout[...] = total(turn).astype(BF16)
            crossing.start()

    pl.semaphore_wait(barrier, len(neighbours))
    g_own(0, 0, to_peer).start()
    g_own(0, 1, to_near).start()
    g_own(0, 2, to_wide).start()
    w_copy(0, 0, w_hbm).start()
    w_copy(0, 1, w_hbm).start()
    g_own(1, 3, to_peer).start()
    g_own(1, 4, to_near).start()
    g_own(1, 5, to_wide).start()
    remote(grad_hbm, gf.at[mp], sib_send.at[me], sib_recv.at[me], to_sibling).start()

    for load in loads:
        load.wait()
    for b in range(2):
        for h in range(2):
            rows, lanes = slice(b * SEQ, (b + 1) * SEQ), slice(h * HD, (h + 1) * HD)
            scores = dot(q_ref[rows, lanes], k_ref[rows, lanes], ((1,), (1,))) * factor
            raised = jnp.exp(scores - jnp.max(scores, axis=-1, keepdims=True))
            attention = raised / jnp.sum(raised, axis=-1, keepdims=True)
            att[b * 2 + h] = attention
            context = dot(attention.astype(BF16), v_ref[rows, lanes])
            ctx_t[lanes, rows] = context.T.astype(BF16)

    w_step(1)
    g_wait(peer, 0)
    g_copy(peer, 0, 6, to_near).start()
    own_partial(me)
    sib_partial(me)
    w_step(2)
    g_wait(near, 0)
    g_wait(near, 1)
    g_copy(near, 1, 7, to_peer).start()
    g_copy(near, 1, 8, to_wide).start()
    g_wait(peer, 1)
    g_copy(peer, 0, 9, to_wide).start()
    g_copy(peer, 1, 10, to_wide).start()
    g_wait(wide, 0)
    g_copy(wide, 0, 11, to_near).start()
    g_wait(wide, 1)
    sib_copy(peer, c).start()
    sib_copy(near, c).start()
    sib_copy(wide, c).start()
    w_step(3)
    own_partial(peer)
    own_partial(near)
    sib_partial(peer)
    sib_partial(near)
    w_step(4)
    g_wait(near_peer, 0)
    g_wait(near_peer, 1)
    sib_copy(near_peer, c).start()
    g_wait(opposite, 1)
    g_copy(opposite, 1, 12, to_peer).start()
    own_partial(near_peer)
    sib_partial(near_peer)
    r_start(0)
    w_step(5)
    own_partial(wide)
    sib_partial(wide)
    g_wait(opposite, 0)
    sib_copy(opposite, c).start()
    own_partial(opposite)
    g_wait(wide_peer, 0)
    g_copy(wide_peer, 0, 13, to_near).start()
    r_step(1, 0)
    w_step(6)
    sib_partial(opposite)
    r_step(2, 0)
    w_step(7)
    g_wait(wide_peer, 1)
    sib_copy(wide_peer, c).start()
    g_wait(opposite_peer, 1)
    g_wait(opposite_peer, 0)
    sib_copy(opposite_peer, c).start()
    own_partial(wide_peer)
    own_partial(opposite_peer)
    r_step(3, 0)
    w_step(8)
    sib_partial(wide_peer)
    sib_partial(opposite_peer)
    r_start(1)
    for offset in (0, 1, -1, 2):
        wx_start(offset)
    r_step(4, 0)
    for offset in (-2, 3, -3, 4):
        wx_start(offset)
    r_step(1, 1)
    r_step(5, 0)
    for offset in (-4, 5, -5, 6):
        wx_start(offset)
    r_step(2, 1)
    r_step(6, 0)
    for offset in (-6, 7, -7, 8):
        wx_start(offset)
    r_step(3, 1)
    r_step(7, 0)
    r_step(4, 1)
    finish(0)
    r_step(5, 1)
    for slot in range(14):
        g_copy(me, 0, slot, to_peer).wait_send()
    each(0, 8, lambda p: sib_copy(p, c).wait_send())
    r_step(6, 1)
    for direction in range(2):
        each(0, (8, 7)[direction], lambda step: w_copy(step, direction).wait_send())
    r_step(7, 1)
    finish(1)
    crossing.wait_recv()
    summed = own_sum[...] + xin[...].astype(F32)
    own_sum[...] = summed
    unscaled = summed * inverse

    def fold(a):
        return a.reshape(COLS // 8, 8, HEADS)

    squares = jnp.sum(fold(unscaled * unscaled), axis=0)
    sizes = jnp.max(fold(jnp.abs(summed)), axis=0)
    stats[0, 0, 0] = squares[:, :128] + squares[:, 128:]
    stats[0, 0, 1] = jnp.maximum(sizes[:, :128], sizes[:, 128:])

    x_core = (xh * 2 + xl) * 2 + c

    def s_targets(turn):
        if turn < 2:
            return [to_dp(xh * NZ + (z + i * 4 ** turn) % NZ) for i in range(1, 4)]
        if turn == 2:
            return [to_mp(((y + i) % NY) * 4 + xl * 2 + c) for i in range(1, 4)]
        found = []
        for i in range(1, 8):
            g = (x_core + i) % 8
            found.append({"dp": (g // 4) * NZ + z, "mp": y * 4 + g % 4})
        return found

    def s_copies(turn):
        return [
            remote(
                stats.at[turn, 0], stats.at[turn, i + 1],
                s_send.at[turn, i], s_recv.at[turn, i], device,
            )
            for i, device in enumerate(s_targets(turn))
        ]

    def s_start(turn):
        for copy in s_copies(turn):
            copy.start()

    def s_finish(turn):
        copies = s_copies(turn)
        for copy in copies:
            copy.wait_recv()
        count = len(copies) + 1
        return jnp.sum(stats[turn, :count, 0], axis=0), jnp.max(stats[turn, :count, 1], axis=0)

    s_start(0)

    each(0, NZ, lambda i: wx_copy(i, 1 - xh).wait_recv())
    acc[...] = jnp.zeros_like(acc)

    def add_context(m):
        rows = wt[m // 8, pl.ds(2 * (m % 8), 2)].reshape(MINE, HEADS)
        acc[...] += dot(gf[m].reshape(TOK, MINE), rows)

    each(0, 16, add_context)
    gc[...] = (acc[...] * scaling).astype(BF16)

    stats[1, 0, 0], stats[1, 0, 1] = s_finish(0)
    s_start(1)

    for b in range(2):
        for h in range(2):
            rows, lanes = slice(b * SEQ, (b + 1) * SEQ), slice(h * HD, (h + 1) * HD)
            attention = att[b * 2 + h]
            grad = gc[rows, lanes]
            gv_ref[rows, lanes] = (dot(attention.T.astype(BF16), grad) * inverse).astype(BF16)
            grad_attention = dot(grad, v_ref[rows, lanes], ((1,), (1,)))
            row_dots = jnp.sum(attention * grad_attention, axis=-1, keepdims=True)
            grad_scores = attention * (grad_attention - row_dots) * factor
            gq_ref[rows, lanes] = (
                dot(grad_scores.astype(BF16), k_ref[rows, lanes]) * inverse
            ).astype(BF16)
            gk_ref[rows, lanes] = (
                dot(grad_scores.T.astype(BF16), q_ref[rows, lanes]) * inverse
            ).astype(BF16)

    stats[2, 0, 0], stats[2, 0, 1] = s_finish(1)
    s_start(2)
    each(0, NZ, lambda i: wx_copy(i, xh).wait_send())
    stats[3, 0, 0], stats[3, 0, 1] = s_finish(2)
    s_start(3)
    for direction in range(2):
        for turn in range(2):
            each(
                0, (8, 7)[direction],
                lambda step: r_copy(step, direction, turn, part.at[0, 0]).wait_send(),
            )
    crossing.wait_send()
    squares, sizes = s_finish(3)
    squares, largest = jnp.sum(squares, keepdims=True), jnp.max(sizes, keepdims=True)
    grad_magnitude = jnp.sqrt(squares / float(H * HD * D) + EPSILON)
    clipping = jnp.minimum(1.0, 1.0 / grad_magnitude)
    gw_ref[...] = (own_sum[...] * inverse * clipping).astype(BF16)
    scalars_ref[0] = jnp.broadcast_to(jnp.log2(OVERFLOW_BOUND / (largest + EPSILON)), (8, 128))
    scalars_ref[1] = jnp.broadcast_to(grad_magnitude, (8, 128))
    for turn in range(4):
        for copy in s_copies(turn):
            copy.wait_send()


def hand_over(gq, gk, gv, gw, scalars, gq_out, gk_out, gv_out, gw_out, headroom, magnitude, sems):
    pairs = ((gq, gq_out), (gk, gk_out), (gv, gv_out), (gw, gw_out))
    copies = [pltpu.make_async_copy(a, b, sems.at[i]) for i, (a, b) in enumerate(pairs)]
    for copy in copies:
        copy.start()
    headroom[0] = jnp.max(scalars[0])
    magnitude[0] = jnp.max(scalars[1])
    for copy in copies:
        copy.wait()


def shards(grad_out, queries, key_rows, value_rows, out_weight, scale_exponent):
    vmem = pl.BlockSpec(memory_space=pltpu.VMEM)
    smem = pl.BlockSpec(memory_space=pltpu.SMEM)
    hbm = pl.BlockSpec(memory_space=pltpu.HBM)
    dma = pltpu.SemaphoreType.DMA
    shape = jax.ShapeDtypeStruct
    results = [shape((TOK, HEADS), BF16)] * 3 + [shape((COLS, HEADS), BF16)]
    outs = pl.pallas_call(
        kernel,
        out_shape=results + [shape((2, 8, 128), F32)],
        in_specs=[smem] + [hbm] * 5,
        out_specs=[vmem] * 5,
        scratch_shapes=[
            pltpu.VMEM((TOK, HEADS), BF16),
            pltpu.VMEM((TOK, HEADS), BF16),
            pltpu.VMEM((TOK, HEADS), BF16),
            dma((5,)),
            pltpu.VMEM((16, 2, SEQ, MINE), BF16),
            pltpu.VMEM((2, NZ, COLS, HEADS), BF16),
            pltpu.VMEM((2, NZ, COLS, HEADS), BF16),
            pltpu.VMEM((2, 8, 2, COLS, HEADS), BF16),
            pltpu.VMEM((COLS, HEADS), BF16),
            pltpu.VMEM((COLS, HEADS), BF16),
            pltpu.VMEM((4, SEQ, SEQ), F32),
            pltpu.VMEM((HEADS, TOK), BF16),
            pltpu.VMEM((TOK, HEADS), F32),
            pltpu.VMEM((TOK, HEADS), BF16),
            pltpu.VMEM((COLS, HEADS), F32),
            pltpu.VMEM((4, 8, 2, 8, 128), F32),
            dma((14,)), dma((8, 2)), dma((8,)), dma((8,)),
            dma((2, 8)), dma((2, 8)), dma((NZ,)), dma((NZ,)),
            dma((2, 8, 2)), dma((2, 8, 2)), dma, dma,
            dma((4, 7)), dma((4, 7)),
        ],
        compiler_params=pltpu.CompilerParams(
            collective_id=0, has_side_effects=True
        ),
    )(
        scale_exponent.reshape(1), grad_out.reshape(2, SEQ, MINE),
        queries, key_rows, value_rows, out_weight.T,
    )
    grad_query, grad_key, grad_value, grad_weight, headroom, magnitude = pl.pallas_call(
        hand_over,
        out_shape=results + [shape((1,), F32)] * 2,
        in_specs=[vmem] * 5,
        out_specs=[hbm] * 4 + [smem] * 2,
        scratch_shapes=[dma((4,))],
    )(*outs)
    return (
        grad_query, grad_key, grad_value, grad_weight.T,
        headroom.reshape(()), magnitude.reshape(()),
    )


def solution(mesh):
    placed = (P("dp", "mp"), P("dp", "mp"), P("dp", "mp"), P("dp", "mp"), P("mp", "dp"), P())
    return jax.shard_map(
        shards,
        mesh=mesh,
        in_specs=placed,
        out_specs=(P("dp", "mp"), P("dp", "mp"), P("dp", "mp"), P("mp", "dp"), P(), P()),
        check_vma=False,
    )
```

```python
import jax
import jax.numpy as jnp
from jax import lax
from jax.experimental import pallas as pl
from jax.experimental.pallas import tpu as pltpu
from jax.sharding import PartitionSpec as P

D = 6144
H = 32
HD = 128
SEQ = 256
NZ = 16
NY = 4
TOK = 512
MINE = 384
HEADS = 256
COLS = 192
CUT = COLS // 2

OVERFLOW_BOUND = 65504.0
EPSILON = 1e-06
MESH = pl.DeviceIdType.MESH
F32 = jnp.float32
BF16 = jnp.bfloat16


def dot(a, b, contract=((1,), (0,))):
    return lax.dot_general(a, b, (contract, ((), ())), preferred_element_type=F32)


def each(first, last, body):
    def step(i, _):
        body(i)
        return 0

    lax.fori_loop(first, last, step, 0)


def remote(source, target, send, recv, device):
    return pltpu.make_async_remote_copy(
        source, target, send, recv, device_id=device, device_id_type=MESH
    )


def kernel(
    exponent_ref, grad_hbm, q_hbm, k_hbm, v_hbm, w_hbm,
    gq_ref, gk_ref, gv_ref, gw_ref, scalars_ref,
    q_ref, k_ref, v_ref, in_sem,
    gf, wt, part, hop, xout, xin, att, ctx_t, acc, gc, own_sum, stats,
    g_send, g_recv, sib_send, sib_recv, w_send, w_recv, wx_send, wx_recv,
    r_send, r_recv, x_send, x_recv, s_send, s_recv,
):
    dp = lax.axis_index("dp")
    mp = lax.axis_index("mp")
    xh, z = dp // NZ, dp % NZ
    y, xl, c = mp // 4, (mp // 2) % 2, mp % 2
    factor = HD ** (-0.5)

    near_y = y + 1 - 2 * (y % 2)
    wide_y, opposite_y = (near_y + 2) % NY, (y + 2) % NY
    me, peer = y * 2 + xl, y * 2 + 1 - xl
    near, near_peer = near_y * 2 + xl, near_y * 2 + 1 - xl
    wide, wide_peer = wide_y * 2 + xl, wide_y * 2 + 1 - xl
    opposite, opposite_peer = opposite_y * 2 + xl, opposite_y * 2 + 1 - xl

    def to_mp(index):
        return {"dp": dp, "mp": index}

    def to_dp(index):
        return {"dp": index, "mp": mp}

    to_near, to_wide = to_mp(near * 2 + c), to_mp(wide * 2 + c)
    to_peer, to_sibling = to_mp(peer * 2 + c), to_mp(me * 2 + 1 - c)
    right, left = to_dp(xh * NZ + (z + 1) % NZ), to_dp(xh * NZ + (z + NZ - 1) % NZ)
    far = to_dp((1 - xh) * NZ + z)

    barrier = pltpu.get_barrier_semaphore()
    neighbours = (to_near, to_wide, to_peer, to_sibling, right, left, far)
    for device in neighbours:
        pl.semaphore_signal(barrier, inc=1, device_id=device, device_id_type=MESH)
    loads = [
        pltpu.make_async_copy(source, target, in_sem.at[i])
        for i, (source, target) in enumerate((
            (q_hbm, q_ref), (k_hbm, k_ref), (v_hbm, v_ref),
            (grad_hbm, gf.at[mp]), (w_hbm, wt.at[xh, z]),
        ))
    ]
    for load in loads:
        load.start()

    exponent = exponent_ref[0]
    scaling = lax.shift_left(jnp.int32(1), exponent).astype(F32)
    inverse = lax.shift_left(jnp.int32(1), 24 - exponent).astype(F32) * (2.0 ** -24)

    def g_copy(p, h, slot, device):
        piece = gf.at[p * 2 + c, h]
        return remote(piece, piece, g_send.at[slot], g_recv.at[p, h], device)

    def g_own(h, slot, device):
        return remote(
            grad_hbm.at[h], gf.at[mp, h], g_send.at[slot], g_recv.at[me, h], device
        )

    def g_wait(p, h):
        g_copy(p, h, 0, to_peer).wait_recv()

    def sib_copy(p, cc):
        piece = gf.at[p * 2 + cc]
        return remote(piece, piece, sib_send.at[p], sib_recv.at[p], to_sibling)

    def w_copy(step, direction, source=None):
        piece = wt.at[xh, (z + NZ - step) % NZ if direction == 0 else (z + step) % NZ]
        return remote(
            piece if source is None else source, piece,
            w_send.at[direction, step], w_recv.at[direction, step],
            right if direction == 0 else left,
        )

    def w_arrived(step, direction):
        index = (z + NZ - step - 1) % NZ if direction == 0 else (z + step + 1) % NZ
        piece = wt.at[xh, index]
        remote(
            piece, piece, w_send.at[direction, step], w_recv.at[direction, step],
            right if direction == 0 else left,
        ).wait_recv()

    def w_step(step):
        for direction in range(2):
            if step <= (8, 7)[direction]:
                w_arrived(step - 1, direction)
            if step < (8, 7)[direction]:
                w_copy(step, direction).start()

    def wx_copy(index, half):
        piece = wt.at[half, index]
        return remote(piece, piece, wx_send.at[index], wx_recv.at[index], far)

    def pair_of(order):
        return (z // 2 + (0, 1, 7, 2, 6, 3, 5, 4)[order]) % 8

    def wx_pair(order):
        for i in range(2):
            wx_copy(2 * pair_of(order) + i, xh).start()

    def add_context(order):
        pair = pair_of(order)
        for i in range(2):
            wx_copy(2 * pair + i, 1 - xh).wait_recv()
        for half in range(2):
            rows = wt[half, pl.ds(2 * pair, 2)].reshape(MINE, HEADS)
            acc[...] += dot(gf[half * 8 + pair].reshape(TOK, MINE), rows)

    def attention_backward(b, h):
        rows, lanes = slice(b * SEQ, (b + 1) * SEQ), slice(h * HD, (h + 1) * HD)
        attention = att[b * 2 + h]
        grad = gc[rows, lanes]
        gv_ref[rows, lanes] = (dot(attention.T.astype(BF16), grad) * inverse).astype(BF16)
        grad_attention = dot(grad, v_ref[rows, lanes], ((1,), (1,)))
        row_dots = jnp.sum(attention * grad_attention, axis=-1, keepdims=True)
        grad_scores = attention * (grad_attention - row_dots) * factor
        gq_ref[rows, lanes] = (
            dot(grad_scores.astype(BF16), k_ref[rows, lanes]) * inverse
        ).astype(BF16)
        gk_ref[rows, lanes] = (
            dot(grad_scores.T.astype(BF16), q_ref[rows, lanes]) * inverse
        ).astype(BF16)

    def partial_of(m):
        block = dot(ctx_t[...], gf[m].reshape(TOK, MINE))
        turned = (block.T * scaling).astype(BF16)
        part[m // 8, 2 * (m % 8)] = turned[:COLS]
        part[m // 8, 2 * (m % 8) + 1] = turned[COLS:]

    def own_partial(p):
        partial_of(p * 2 + c)

    def sib_partial(p):
        sib_copy(p, 1 - c).wait_recv()
        partial_of(p * 2 + 1 - c)

    first = y // 2

    def half_of(turn):
        return first if turn == 0 else 1 - first

    def r_copy(step, direction, turn, piece, source):
        return remote(
            source, hop.at[direction, step, turn, piece],
            r_send.at[direction, step, turn, piece], r_recv.at[direction, step, turn, piece],
            right if direction == 0 else left,
        )

    def r_part(step, direction, turn, piece):
        dest = (z + 8 - step) % NZ if direction == 0 else (z + NZ - 7 + step) % NZ
        return part.at[half_of(turn), dest, piece * CUT : (piece + 1) * CUT]

    def r_start(turn):
        for piece in range(2):
            for direction in range(2):
                r_copy(0, direction, turn, piece, r_part(0, direction, turn, piece)).start()

    def r_arrived(step, direction, turn, piece):
        r_copy(step, direction, turn, piece, hop.at[direction, step, turn, piece]).wait_recv()

    def r_step(step, turn):
        for piece in range(2):
            for direction in range(2):
                if step < (8, 7)[direction]:
                    slot = hop.at[direction, step - 1, turn, piece]
                    r_arrived(step - 1, direction, turn, piece)
                    slot[...] = (
                        slot[...].astype(F32) + r_part(step, direction, turn, piece)[...].astype(F32)
                    ).astype(BF16)
                    r_copy(step, direction, turn, piece, slot).start()

    def total(turn):
        return (
            part[half_of(turn), z].astype(F32)
            + hop[0, 7, turn].reshape(COLS, HEADS).astype(F32)
            + hop[1, 6, turn].reshape(COLS, HEADS).astype(F32)
        )

    crossing = remote(xout, xin, x_send, x_recv, far)

    def finish(turn):
        for piece in range(2):
            r_arrived(6, 1, turn, piece)
            r_arrived(7, 0, turn, piece)

        @pl.when(xh == half_of(turn))
        def _():
            own_sum[...] = total(turn)

        @pl.when(xh != half_of(turn))
        def _():
            xout[...] = total(turn).astype(BF16)
            crossing.start()

    pl.semaphore_wait(barrier, len(neighbours))
    own_to_peer = [g_own(0, 0, to_peer), g_own(1, 3, to_peer)]
    own_to_near = [g_own(0, 1, to_near), g_own(1, 4, to_near)]
    own_to_wide = [g_own(0, 2, to_wide), g_own(1, 5, to_wide)]
    peer_to_near, near_to_peer = g_copy(peer, 0, 6, to_near), g_copy(near, 1, 7, to_peer)
    near_to_wide = g_copy(near, 1, 8, to_wide)
    peer_to_wide = [g_copy(peer, 0, 9, to_wide), g_copy(peer, 1, 10, to_wide)]
    wide_to_near, opposite_to_peer = g_copy(wide, 0, 11, to_near), g_copy(opposite, 1, 12, to_peer)
    wide_peer_to_near = g_copy(wide_peer, 0, 13, to_near)

    own_to_near[0].start()
    own_to_peer[0].start()
    own_to_wide[0].start()
    w_copy(0, 0, w_hbm).start()
    w_copy(0, 1, w_hbm).start()
    remote(grad_hbm, gf.at[mp], sib_send.at[me], sib_recv.at[me], to_sibling).start()

    for load in loads:
        load.wait()
    for b in range(2):
        for h in range(2):
            rows, lanes = slice(b * SEQ, (b + 1) * SEQ), slice(h * HD, (h + 1) * HD)
            scores = dot(q_ref[rows, lanes], k_ref[rows, lanes], ((1,), (1,))) * factor
            raised = jnp.exp(scores - jnp.max(scores, axis=-1, keepdims=True))
            attention = raised / jnp.sum(raised, axis=-1, keepdims=True)
            att[b * 2 + h] = attention
            context = dot(attention.astype(BF16), v_ref[rows, lanes])
            ctx_t[lanes, rows] = context.T.astype(BF16)

    for sends in (own_to_near, own_to_peer, own_to_wide):
        sends[0].wait_send()
        sends[1].start()
    w_step(1)
    own_partial(me)
    sib_partial(me)
    w_step(2)
    g_wait(peer, 0)
    own_to_near[1].wait_send()
    peer_to_near.start()
    g_wait(near, 1)
    own_to_peer[1].wait_send()
    near_to_peer.start()
    own_to_wide[1].wait_send()
    near_to_wide.start()
    g_wait(peer, 1)
    sib_copy(peer, c).start()
    g_wait(near, 0)
    sib_copy(near, c).start()
    own_partial(peer)
    own_partial(near)
    g_wait(wide, 0)
    g_wait(wide, 1)
    sib_copy(wide, c).start()
    sib_partial(peer)
    sib_partial(near)
    w_step(3)
    peer_to_near.wait_send()
    wide_to_near.start()
    near_to_wide.wait_send()
    peer_to_wide[0].start()
    g_wait(near_peer, 0)
    g_wait(near_peer, 1)
    sib_copy(near_peer, c).start()
    g_wait(opposite, 1)
    near_to_peer.wait_send()
    opposite_to_peer.start()
    own_partial(near_peer)
    sib_partial(near_peer)
    r_start(0)
    w_step(4)
    own_partial(wide)
    sib_partial(wide)
    wide_to_near.wait_send()
    g_wait(wide_peer, 0)
    wide_peer_to_near.start()
    peer_to_wide[0].wait_send()
    peer_to_wide[1].start()
    g_wait(opposite, 0)
    sib_copy(opposite, c).start()
    wx_pair(0)
    r_step(1, 0)
    own_partial(opposite)
    w_step(5)
    sib_partial(opposite)
    g_wait(wide_peer, 1)
    sib_copy(wide_peer, c).start()
    g_wait(opposite_peer, 1)
    g_wait(opposite_peer, 0)
    sib_copy(opposite_peer, c).start()
    r_step(2, 0)
    own_partial(wide_peer)
    own_partial(opposite_peer)
    sib_partial(wide_peer)
    sib_partial(opposite_peer)
    r_start(1)
    wx_pair(1)
    w_step(6)
    r_step(3, 0)
    r_step(1, 1)
    wx_pair(2)
    w_step(7)
    r_step(4, 0)
    r_step(2, 1)
    w_step(8)
    wx_pair(3)
    wx_pair(4)
    acc[...] = jnp.zeros_like(acc)
    r_step(5, 0)
    r_step(3, 1)
    wx_pair(5)
    wx_pair(6)
    add_context(0)
    r_step(6, 0)
    r_step(4, 1)
    wx_pair(7)
    add_context(1)
    r_step(7, 0)
    r_step(5, 1)
    add_context(2)
    add_context(3)
    finish(0)
    r_step(6, 1)
    for copy in (peer_to_wide[1], opposite_to_peer, wide_peer_to_near):
        copy.wait_send()
    each(0, 8, lambda p: sib_copy(p, c).wait_send())
    add_context(4)
    add_context(5)
    r_step(7, 1)
    for direction in range(2):
        each(0, (8, 7)[direction], lambda step: w_copy(step, direction).wait_send())
    add_context(6)
    finish(1)
    add_context(7)
    gc[...] = (acc[...] * scaling).astype(BF16)
    attention_backward(0, 0)
    attention_backward(0, 1)
    crossing.wait_recv()
    summed = own_sum[...] + xin[...].astype(F32)
    own_sum[...] = summed
    unscaled = summed * inverse

    def fold(a):
        return a.reshape(COLS // 8, 8, HEADS)

    squares = jnp.sum(fold(unscaled * unscaled), axis=0)
    sizes = jnp.max(fold(jnp.abs(summed)), axis=0)
    stats[0, 0, 0] = squares[:, :128] + squares[:, 128:]
    stats[0, 0, 1] = jnp.maximum(sizes[:, :128], sizes[:, 128:])

    x_core = (xh * 2 + xl) * 2 + c

    def s_targets(turn):
        if turn < 2:
            return [to_dp(xh * NZ + (z + i * 4 ** turn) % NZ) for i in range(1, 4)]
        if turn == 2:
            return [to_mp(((y + i) % NY) * 4 + xl * 2 + c) for i in range(1, 4)]
        found = []
        for i in range(1, 8):
            g = (x_core + i) % 8
            found.append({"dp": (g // 4) * NZ + z, "mp": y * 4 + g % 4})
        return found

    def s_copies(turn):
        return [
            remote(
                stats.at[turn, 0], stats.at[turn, i + 1],
                s_send.at[turn, i], s_recv.at[turn, i], device,
            )
            for i, device in enumerate(s_targets(turn))
        ]

    def s_start(turn):
        for copy in s_copies(turn):
            copy.start()

    def s_finish(turn):
        copies = s_copies(turn)
        for copy in copies:
            copy.wait_recv()
        count = len(copies) + 1
        return jnp.sum(stats[turn, :count, 0], axis=0), jnp.max(stats[turn, :count, 1], axis=0)

    s_start(0)

    attention_backward(1, 0)
    stats[1, 0, 0], stats[1, 0, 1] = s_finish(0)
    s_start(1)
    each(0, NZ, lambda i: wx_copy(i, xh).wait_send())
    attention_backward(1, 1)
    stats[2, 0, 0], stats[2, 0, 1] = s_finish(1)
    s_start(2)
    stats[3, 0, 0], stats[3, 0, 1] = s_finish(2)
    s_start(3)
    for direction in range(2):
        for turn in range(2):
            each(
                0, (8, 7)[direction],
                lambda step: [
                    r_copy(step, direction, turn, piece, part.at[0, 0, :CUT]).wait_send()
                    for piece in range(2)
                ],
            )
    crossing.wait_send()
    squares, sizes = s_finish(3)
    squares, largest = jnp.sum(squares, keepdims=True), jnp.max(sizes, keepdims=True)
    grad_magnitude = jnp.sqrt(squares / float(H * HD * D) + EPSILON)
    clipping = jnp.minimum(1.0, 1.0 / grad_magnitude)
    gw_ref[...] = (own_sum[...] * inverse * clipping).astype(BF16)
    scalars_ref[0] = jnp.broadcast_to(jnp.log2(OVERFLOW_BOUND / (largest + EPSILON)), (8, 128))
    scalars_ref[1] = jnp.broadcast_to(grad_magnitude, (8, 128))
    for turn in range(4):
        for copy in s_copies(turn):
            copy.wait_send()


def hand_over(gq, gk, gv, gw, scalars, gq_out, gk_out, gv_out, gw_out, headroom, magnitude, sems):
    pairs = ((gq, gq_out), (gk, gk_out), (gv, gv_out), (gw, gw_out))
    copies = [pltpu.make_async_copy(a, b, sems.at[i]) for i, (a, b) in enumerate(pairs)]
    for copy in copies:
        copy.start()
    headroom[0] = jnp.max(scalars[0])
    magnitude[0] = jnp.max(scalars[1])
    for copy in copies:
        copy.wait()


def shards(grad_out, queries, key_rows, value_rows, out_weight, scale_exponent):
    vmem = pl.BlockSpec(memory_space=pltpu.VMEM)
    smem = pl.BlockSpec(memory_space=pltpu.SMEM)
    hbm = pl.BlockSpec(memory_space=pltpu.HBM)
    dma = pltpu.SemaphoreType.DMA
    shape = jax.ShapeDtypeStruct
    results = [shape((TOK, HEADS), BF16)] * 3 + [shape((COLS, HEADS), BF16)]
    outs = pl.pallas_call(
        kernel,
        out_shape=results + [shape((2, 8, 128), F32)],
        in_specs=[smem] + [hbm] * 5,
        out_specs=[vmem] * 5,
        scratch_shapes=[
            pltpu.VMEM((TOK, HEADS), BF16),
            pltpu.VMEM((TOK, HEADS), BF16),
            pltpu.VMEM((TOK, HEADS), BF16),
            dma((5,)),
            pltpu.VMEM((16, 2, SEQ, MINE), BF16),
            pltpu.VMEM((2, NZ, COLS, HEADS), BF16),
            pltpu.VMEM((2, NZ, COLS, HEADS), BF16),
            pltpu.VMEM((2, 8, 2, 2, CUT, HEADS), BF16),
            pltpu.VMEM((COLS, HEADS), BF16),
            pltpu.VMEM((COLS, HEADS), BF16),
            pltpu.VMEM((4, SEQ, SEQ), F32),
            pltpu.VMEM((HEADS, TOK), BF16),
            pltpu.VMEM((TOK, HEADS), F32),
            pltpu.VMEM((TOK, HEADS), BF16),
            pltpu.VMEM((COLS, HEADS), F32),
            pltpu.VMEM((4, 8, 2, 8, 128), F32),
            dma((14,)), dma((8, 2)), dma((8,)), dma((8,)),
            dma((2, 8)), dma((2, 8)), dma((NZ,)), dma((NZ,)),
            dma((2, 8, 2, 2)), dma((2, 8, 2, 2)), dma, dma,
            dma((4, 7)), dma((4, 7)),
        ],
        compiler_params=pltpu.CompilerParams(
            collective_id=0, has_side_effects=True
        ),
    )(
        scale_exponent.reshape(1), grad_out.reshape(2, SEQ, MINE),
        queries, key_rows, value_rows, out_weight.T,
    )
    grad_query, grad_key, grad_value, grad_weight, headroom, magnitude = pl.pallas_call(
        hand_over,
        out_shape=results + [shape((1,), F32)] * 2,
        in_specs=[vmem] * 5,
        out_specs=[hbm] * 4 + [smem] * 2,
        scratch_shapes=[dma((4,))],
    )(*outs)
    return (
        grad_query, grad_key, grad_value, grad_weight.T,
        headroom.reshape(()), magnitude.reshape(()),
    )


def solution(mesh):
    placed = (P("dp", "mp"), P("dp", "mp"), P("dp", "mp"), P("dp", "mp"), P("mp", "dp"), P())
    return jax.shard_map(
        shards,
        mesh=mesh,
        in_specs=placed,
        out_specs=(P("dp", "mp"), P("dp", "mp"), P("dp", "mp"), P("mp", "dp"), P(), P()),
        check_vma=False,
    )
```

```python
import jax
import jax.numpy as jnp
from jax import lax
from jax.experimental import pallas as pl
from jax.experimental.pallas import tpu as pltpu
from jax.sharding import PartitionSpec as P

D = 6144
H = 32
HD = 128
SEQ = 256
NZ = 16
NY = 4
TOK = 512
MINE = 384
HEADS = 256
COLS = 192
CUT = COLS // 2

OVERFLOW_BOUND = 65504.0
EPSILON = 1e-06
MESH = pl.DeviceIdType.MESH
F32 = jnp.float32
BF16 = jnp.bfloat16


def dot(a, b, contract=((1,), (0,))):
    return lax.dot_general(a, b, (contract, ((), ())), preferred_element_type=F32)


def each(first, last, body):
    def step(i, _):
        body(i)
        return 0

    lax.fori_loop(first, last, step, 0)


def wrap(a, n):
    return lax.rem(a, jnp.int32(n))


def over(a, n):
    return lax.div(a, jnp.int32(n))


def remote(source, target, send, recv, device):
    return pltpu.make_async_remote_copy(
        source, target, send, recv, device_id=device, device_id_type=MESH
    )


def kernel(
    exponent_ref, grad_hbm, q_hbm, k_hbm, v_hbm, w_hbm,
    gq_hbm, gk_hbm, gv_hbm, gw_ref, scalars_ref,
    q_ref, k_ref, v_ref, in_sem, gq_ref, gk_ref, gv_ref, out_sem,
    gf, wt, part, hop, xout, xin, att, ctx_t, acc, gc, own_sum, stats,
    g_send, g_recv, sib_send, sib_recv, w_send, w_recv, wx_send, wx_recv,
    r_send, r_recv, x_send, x_recv, s_send, s_recv,
):
    dp = lax.axis_index("dp")
    mp = lax.axis_index("mp")
    xh, z = over(dp, NZ), wrap(dp, NZ)
    y, xl, c = over(mp, 4), wrap(over(mp, 2), 2), wrap(mp, 2)
    factor = HD ** (-0.5)

    near_y = y + 1 - 2 * wrap(y, 2)
    wide_y, opposite_y = wrap(near_y + 2, NY), wrap(y + 2, NY)
    me, peer = y * 2 + xl, y * 2 + 1 - xl
    near, near_peer = near_y * 2 + xl, near_y * 2 + 1 - xl
    wide, wide_peer = wide_y * 2 + xl, wide_y * 2 + 1 - xl
    opposite, opposite_peer = opposite_y * 2 + xl, opposite_y * 2 + 1 - xl

    def to_mp(index):
        return {"dp": dp, "mp": index}

    def to_dp(index):
        return {"dp": index, "mp": mp}

    to_near, to_wide = to_mp(near * 2 + c), to_mp(wide * 2 + c)
    to_peer, to_sibling = to_mp(peer * 2 + c), to_mp(me * 2 + 1 - c)
    right = to_dp(xh * NZ + wrap(z + 1, NZ))
    left = to_dp(xh * NZ + wrap(z + NZ - 1, NZ))
    far = to_dp((1 - xh) * NZ + z)

    barrier = pltpu.get_barrier_semaphore()
    neighbours = (to_near, to_wide, to_peer, to_sibling, right, left, far)
    for device in neighbours:
        pl.semaphore_signal(barrier, inc=1, device_id=device, device_id_type=MESH)
    loads = [
        pltpu.make_async_copy(source, target, in_sem.at[i])
        for i, (source, target) in enumerate((
            (q_hbm, q_ref), (k_hbm, k_ref), (v_hbm, v_ref),
            (grad_hbm, gf.at[mp]), (w_hbm, wt.at[xh, z]),
        ))
    ]
    for load in loads:
        load.start()

    exponent = exponent_ref[0]
    scaling = lax.shift_left(jnp.int32(1), exponent).astype(F32)
    inverse = lax.shift_left(jnp.int32(1), 24 - exponent).astype(F32) * (2.0 ** -24)

    def g_copy(p, h, slot, device):
        piece = gf.at[p * 2 + c, h]
        return remote(piece, piece, g_send.at[slot], g_recv.at[p, h], device)

    def g_own(h, slot, device):
        return remote(
            grad_hbm.at[h], gf.at[mp, h], g_send.at[slot], g_recv.at[me, h], device
        )

    def g_wait(p, h):
        g_copy(p, h, 0, to_peer).wait_recv()

    def sib_copy(p, cc):
        piece = gf.at[p * 2 + cc]
        return remote(piece, piece, sib_send.at[p], sib_recv.at[p], to_sibling)

    def w_copy(step, direction, source=None):
        piece = wt.at[xh, wrap(z + NZ - step if direction == 0 else z + step, NZ)]
        return remote(
            piece if source is None else source, piece,
            w_send.at[direction, step], w_recv.at[direction, step],
            right if direction == 0 else left,
        )

    def w_arrived(step, direction):
        index = wrap(z + NZ - step - 1 if direction == 0 else z + step + 1, NZ)
        piece = wt.at[xh, index]
        remote(
            piece, piece, w_send.at[direction, step], w_recv.at[direction, step],
            right if direction == 0 else left,
        ).wait_recv()

    def w_step(step):
        for direction in range(2):
            if step <= (8, 7)[direction]:
                w_arrived(step - 1, direction)
            if step < (8, 7)[direction]:
                w_copy(step, direction).start()

    def wx_copy(index, half):
        piece = wt.at[half, index]
        return remote(piece, piece, wx_send.at[index], wx_recv.at[index], far)

    def pair_of(order):
        return wrap(over(z, 2) + (0, 1, 7, 2, 6, 3, 5, 4)[order], 8)

    def wx_pair(order):
        for i in range(2):
            wx_copy(2 * pair_of(order) + i, xh).start()

    def add_context(order):
        pair = pair_of(order)
        for i in range(2):
            wx_copy(2 * pair + i, 1 - xh).wait_recv()
        for half in range(2):
            rows = wt[half, pl.ds(2 * pair, 2)].reshape(MINE, HEADS)
            acc[...] += dot(gf[half * 8 + pair].reshape(TOK, MINE), rows)

    def attention_backward(b, h):
        rows, lanes = slice(b * SEQ, (b + 1) * SEQ), slice(h * HD, (h + 1) * HD)
        attention = att[b * 2 + h]
        grad = gc[rows, lanes]
        gv_ref[rows, lanes] = (dot(attention.T.astype(BF16), grad) * inverse).astype(BF16)
        grad_attention = dot(grad, v_ref[rows, lanes], ((1,), (1,)))
        row_dots = jnp.sum(attention * grad_attention, axis=-1, keepdims=True)
        grad_scores = attention * (grad_attention - row_dots) * factor
        gq_ref[rows, lanes] = (
            dot(grad_scores.astype(BF16), k_ref[rows, lanes]) * inverse
        ).astype(BF16)
        gk_ref[rows, lanes] = (
            dot(grad_scores.T.astype(BF16), q_ref[rows, lanes]) * inverse
        ).astype(BF16)

    def partial_of(m):
        block = dot(ctx_t[...], gf[m].reshape(TOK, MINE))
        turned = (block.T * scaling).astype(BF16)
        half, pair = over(m, 8), wrap(m, 8)
        part[half, 2 * pair] = turned[:COLS]
        part[half, 2 * pair + 1] = turned[COLS:]

    def own_partial(p):
        partial_of(p * 2 + c)

    def sib_partial(p):
        sib_copy(p, 1 - c).wait_recv()
        partial_of(p * 2 + 1 - c)

    first = over(y, 2)

    def half_of(turn):
        return first if turn == 0 else 1 - first

    def r_copy(step, direction, turn, piece, source):
        return remote(
            source, hop.at[direction, step, turn, piece],
            r_send.at[direction, step, turn, piece], r_recv.at[direction, step, turn, piece],
            right if direction == 0 else left,
        )

    def r_part(step, direction, turn, piece):
        dest = wrap(z + 8 - step if direction == 0 else z + NZ - 7 + step, NZ)
        return part.at[half_of(turn), dest, piece * CUT : (piece + 1) * CUT]

    def r_start(turn):
        for piece in range(2):
            for direction in range(2):
                r_copy(0, direction, turn, piece, r_part(0, direction, turn, piece)).start()

    def r_arrived(step, direction, turn, piece):
        r_copy(step, direction, turn, piece, hop.at[direction, step, turn, piece]).wait_recv()

    def r_step(step, turn):
        for piece in range(2):
            for direction in range(2):
                if step < (8, 7)[direction]:
                    slot = hop.at[direction, step - 1, turn, piece]
                    r_arrived(step - 1, direction, turn, piece)
                    slot[...] = (
                        slot[...].astype(F32) + r_part(step, direction, turn, piece)[...].astype(F32)
                    ).astype(BF16)
                    r_copy(step, direction, turn, piece, slot).start()

    def total(turn, piece):
        return (
            r_part(8, 0, turn, piece)[...].astype(F32)
            + hop[0, 7, turn, piece].astype(F32) + hop[1, 6, turn, piece].astype(F32)
        )

    def crossing(piece):
        return remote(xout.at[piece], xin.at[piece], x_send.at[piece], x_recv.at[piece], far)

    def finish(turn):
        for piece in range(2):
            r_arrived(7, 0, turn, piece)
            r_arrived(6, 1, turn, piece)

            @pl.when(xh == half_of(turn))
            def _():
                own_sum[piece] = total(turn, piece)

            @pl.when(xh != half_of(turn))
            def _():
                xout[piece] = total(turn, piece).astype(BF16)
                crossing(piece).start()

    pl.semaphore_wait(barrier, len(neighbours))
    own_to_peer = [g_own(0, 0, to_peer), g_own(1, 3, to_peer)]
    own_to_near = [g_own(0, 1, to_near), g_own(1, 4, to_near)]
    own_to_wide = [g_own(0, 2, to_wide), g_own(1, 5, to_wide)]
    peer_to_near, near_to_peer = g_copy(peer, 0, 6, to_near), g_copy(near, 1, 7, to_peer)
    near_to_wide = g_copy(near, 1, 8, to_wide)
    peer_to_wide = [g_copy(peer, 0, 9, to_wide), g_copy(peer, 1, 10, to_wide)]
    wide_to_near, opposite_to_peer = g_copy(wide, 0, 11, to_near), g_copy(opposite, 1, 12, to_peer)
    wide_peer_to_near = g_copy(wide_peer, 0, 13, to_near)

    own_to_near[0].start()
    own_to_peer[0].start()
    own_to_wide[0].start()
    w_copy(0, 0, w_hbm).start()
    w_copy(0, 1, w_hbm).start()
    remote(grad_hbm, gf.at[mp], sib_send.at[me], sib_recv.at[me], to_sibling).start()

    for load in loads:
        load.wait()
    for b in range(2):
        for h in range(2):
            rows, lanes = slice(b * SEQ, (b + 1) * SEQ), slice(h * HD, (h + 1) * HD)
            scores = dot(q_ref[rows, lanes], k_ref[rows, lanes], ((1,), (1,))) * factor
            raised = jnp.exp(scores - jnp.max(scores, axis=-1, keepdims=True))
            attention = raised / jnp.sum(raised, axis=-1, keepdims=True)
            att[b * 2 + h] = attention
            context = dot(attention.astype(BF16), v_ref[rows, lanes])
            ctx_t[lanes, rows] = context.T.astype(BF16)

    for sends in (own_to_near, own_to_peer, own_to_wide):
        sends[0].wait_send()
        sends[1].start()
    w_step(1)
    own_partial(me)
    sib_partial(me)
    w_step(2)
    g_wait(peer, 0)
    own_to_near[1].wait_send()
    peer_to_near.start()
    g_wait(near, 1)
    own_to_peer[1].wait_send()
    near_to_peer.start()
    own_to_wide[1].wait_send()
    near_to_wide.start()
    g_wait(peer, 1)
    sib_copy(peer, c).start()
    g_wait(near, 0)
    sib_copy(near, c).start()
    own_partial(peer)
    own_partial(near)
    g_wait(wide, 0)
    g_wait(wide, 1)
    sib_copy(wide, c).start()
    sib_partial(peer)
    sib_partial(near)
    w_step(3)
    peer_to_near.wait_send()
    wide_to_near.start()
    near_to_wide.wait_send()
    peer_to_wide[0].start()
    g_wait(near_peer, 0)
    g_wait(near_peer, 1)
    sib_copy(near_peer, c).start()
    g_wait(opposite, 1)
    near_to_peer.wait_send()
    opposite_to_peer.start()
    own_partial(near_peer)
    sib_partial(near_peer)
    r_start(0)
    w_step(4)
    own_partial(wide)
    sib_partial(wide)
    wide_to_near.wait_send()
    g_wait(wide_peer, 0)
    wide_peer_to_near.start()
    peer_to_wide[0].wait_send()
    peer_to_wide[1].start()
    g_wait(opposite, 0)
    sib_copy(opposite, c).start()
    wx_pair(0)
    r_step(1, 0)
    own_partial(opposite)
    w_step(5)
    sib_partial(opposite)
    g_wait(wide_peer, 1)
    sib_copy(wide_peer, c).start()
    g_wait(opposite_peer, 1)
    g_wait(opposite_peer, 0)
    sib_copy(opposite_peer, c).start()
    r_step(2, 0)
    own_partial(wide_peer)
    own_partial(opposite_peer)
    sib_partial(wide_peer)
    sib_partial(opposite_peer)
    r_start(1)
    wx_pair(1)
    w_step(6)
    r_step(3, 0)
    r_step(1, 1)
    wx_pair(2)
    w_step(7)
    r_step(4, 0)
    r_step(2, 1)
    w_step(8)
    wx_pair(3)
    wx_pair(4)
    acc[...] = jnp.zeros_like(acc)
    r_step(5, 0)
    r_step(3, 1)
    wx_pair(5)
    wx_pair(6)
    add_context(0)
    r_step(6, 0)
    r_step(4, 1)
    wx_pair(7)
    add_context(1)
    r_step(7, 0)
    r_step(5, 1)
    add_context(2)
    add_context(3)
    finish(0)
    r_step(6, 1)
    for copy in (peer_to_wide[1], opposite_to_peer, wide_peer_to_near):
        copy.wait_send()
    each(0, 8, lambda p: sib_copy(p, c).wait_send())
    add_context(4)
    add_context(5)
    r_step(7, 1)
    for direction in range(2):
        each(0, (8, 7)[direction], lambda step: w_copy(step, direction).wait_send())
    add_context(6)
    finish(1)
    add_context(7)
    gc[...] = (acc[...] * scaling).astype(BF16)
    attention_backward(0, 0)
    attention_backward(0, 1)
    for piece in range(2):
        crossing(piece).wait_recv()
        own_sum[piece] += xin[piece].astype(F32)
    summed = own_sum[...].reshape(COLS, HEADS)
    unscaled = summed * inverse

    def fold(a):
        return a.reshape(COLS // 8, 8, HEADS)

    squares = jnp.sum(fold(unscaled * unscaled), axis=0)
    sizes = jnp.max(fold(jnp.abs(summed)), axis=0)
    stats[0, 0, 0] = squares[:, :128] + squares[:, 128:]
    stats[0, 0, 1] = jnp.maximum(sizes[:, :128], sizes[:, 128:])

    x_core = (xh * 2 + xl) * 2 + c

    def s_targets(turn):
        if turn < 2:
            return [to_dp(xh * NZ + wrap(z + i * 4 ** turn, NZ)) for i in (2, 3, 1)]
        if turn == 2:
            return [to_mp(wrap(y + i, NY) * 4 + xl * 2 + c) for i in (2, 1, 3)]
        found = []
        for i in (4, 5, 3, 2, 6, 1, 7):
            g = wrap(x_core + i, 8)
            found.append({"dp": over(g, 4) * NZ + z, "mp": y * 4 + wrap(g, 4)})
        return found

    def s_copies(turn):
        return [
            remote(
                stats.at[turn, 0], stats.at[turn, i + 1],
                s_send.at[turn, i], s_recv.at[turn, i], device,
            )
            for i, device in enumerate(s_targets(turn))
        ]

    def s_start(turn):
        for copy in s_copies(turn):
            copy.start()

    def s_finish(turn):
        copies = s_copies(turn)
        for copy in copies:
            copy.wait_recv()
        count = len(copies) + 1
        return jnp.sum(stats[turn, :count, 0], axis=0), jnp.max(stats[turn, :count, 1], axis=0)

    s_start(0)

    attention_backward(1, 0)
    stats[1, 0, 0], stats[1, 0, 1] = s_finish(0)
    s_start(1)
    each(0, NZ, lambda i: wx_copy(i, xh).wait_send())
    attention_backward(1, 1)
    stores = [
        pltpu.make_async_copy(source, target, out_sem.at[i])
        for i, (source, target) in enumerate(
            ((gq_ref, gq_hbm), (gk_ref, gk_hbm), (gv_ref, gv_hbm))
        )
    ]
    for store in stores:
        store.start()
    stats[2, 0, 0], stats[2, 0, 1] = s_finish(1)
    s_start(2)
    stats[3, 0, 0], stats[3, 0, 1] = s_finish(2)
    s_start(3)
    for direction in range(2):
        for turn in range(2):
            each(
                0, (8, 7)[direction],
                lambda step: [
                    r_copy(step, direction, turn, piece, part.at[0, 0, :CUT]).wait_send()
                    for piece in range(2)
                ],
            )
    for piece in range(2):
        crossing(piece).wait_send()
    for store in stores:
        store.wait()
    for turn in range(3):
        for copy in s_copies(turn):
            copy.wait_send()
    squares, sizes = s_finish(3)
    squares, largest = jnp.sum(squares, keepdims=True), jnp.max(sizes, keepdims=True)
    grad_magnitude = jnp.sqrt(squares / float(H * HD * D) + EPSILON)
    clipping = jnp.minimum(1.0, 1.0 / grad_magnitude)
    gw_ref[...] = (own_sum[...].reshape(COLS, HEADS) * inverse * clipping).astype(BF16)
    scalars_ref[0] = jnp.broadcast_to(jnp.log2(OVERFLOW_BOUND / (largest + EPSILON)), (8, 128))
    scalars_ref[1] = jnp.broadcast_to(grad_magnitude, (8, 128))
    for copy in s_copies(3):
        copy.wait_send()


def hand_over(gq, gk, gv, gw, scalars, gq_out, gk_out, gv_out, gw_out, headroom, magnitude, sems):
    pairs = ((gq, gq_out), (gk, gk_out), (gv, gv_out), (gw, gw_out))
    copies = [pltpu.make_async_copy(a, b, sems.at[i]) for i, (a, b) in enumerate(pairs)]
    for copy in copies:
        copy.start()
    headroom[0] = jnp.max(scalars[0])
    magnitude[0] = jnp.max(scalars[1])
    for copy in copies:
        copy.wait()


def shards(grad_out, queries, key_rows, value_rows, out_weight, scale_exponent):
    vmem = pl.BlockSpec(memory_space=pltpu.VMEM)
    smem = pl.BlockSpec(memory_space=pltpu.SMEM)
    hbm = pl.BlockSpec(memory_space=pltpu.HBM)
    dma = pltpu.SemaphoreType.DMA
    shape = jax.ShapeDtypeStruct
    results = [shape((TOK, HEADS), BF16)] * 3 + [shape((COLS, HEADS), BF16)]
    outs = pl.pallas_call(
        kernel,
        out_shape=results + [shape((2, 8, 128), F32)],
        in_specs=[smem] + [hbm] * 5,
        out_specs=[hbm] * 3 + [vmem] * 2,
        scratch_shapes=[
            pltpu.VMEM((TOK, HEADS), BF16),
            pltpu.VMEM((TOK, HEADS), BF16),
            pltpu.VMEM((TOK, HEADS), BF16),
            dma((5,)),
            pltpu.VMEM((TOK, HEADS), BF16),
            pltpu.VMEM((TOK, HEADS), BF16),
            pltpu.VMEM((TOK, HEADS), BF16),
            dma((3,)),
            pltpu.VMEM((16, 2, SEQ, MINE), BF16),
            pltpu.VMEM((2, NZ, COLS, HEADS), BF16),
            pltpu.VMEM((2, NZ, COLS, HEADS), BF16),
            pltpu.VMEM((2, 8, 2, 2, CUT, HEADS), BF16),
            pltpu.VMEM((2, CUT, HEADS), BF16),
            pltpu.VMEM((2, CUT, HEADS), BF16),
            pltpu.VMEM((4, SEQ, SEQ), F32),
            pltpu.VMEM((HEADS, TOK), BF16),
            pltpu.VMEM((TOK, HEADS), F32),
            pltpu.VMEM((TOK, HEADS), BF16),
            pltpu.VMEM((2, CUT, HEADS), F32),
            pltpu.VMEM((4, 8, 2, 8, 128), F32),
            dma((14,)), dma((8, 2)), dma((8,)), dma((8,)),
            dma((2, 8)), dma((2, 8)), dma((NZ,)), dma((NZ,)),
            dma((2, 8, 2, 2)), dma((2, 8, 2, 2)), dma((2,)), dma((2,)),
            dma((4, 7)), dma((4, 7)),
        ],
        compiler_params=pltpu.CompilerParams(
            collective_id=0, has_side_effects=True
        ),
    )(
        scale_exponent.reshape(1), grad_out.reshape(2, SEQ, MINE),
        queries, key_rows, value_rows, out_weight.T,
    )
    grad_query, grad_key, grad_value, grad_weight, headroom, magnitude = pl.pallas_call(
        hand_over,
        out_shape=results + [shape((1,), F32)] * 2,
        in_specs=[vmem] * 5,
        out_specs=[hbm] * 4 + [smem] * 2,
        scratch_shapes=[dma((4,))],
    )(*outs)
    return (
        grad_query, grad_key, grad_value, grad_weight.T,
        headroom.reshape(()), magnitude.reshape(()),
    )


def solution(mesh):
    placed = (P("dp", "mp"), P("dp", "mp"), P("dp", "mp"), P("dp", "mp"), P("mp", "dp"), P())
    return jax.shard_map(
        shards,
        mesh=mesh,
        in_specs=placed,
        out_specs=(P("dp", "mp"), P("dp", "mp"), P("dp", "mp"), P("mp", "dp"), P(), P()),
        check_vma=False,
    )
```

```python
import jax
import jax.numpy as jnp
from jax import lax
from jax.experimental import pallas as pl
from jax.experimental.pallas import tpu as pltpu
from jax.sharding import PartitionSpec as P

D = 6144
H = 32
HD = 128
SEQ = 256
NZ = 16
NY = 4
TOK = 512
MINE = 384
HEADS = 256
COLS = 192
CUT = COLS // 2

OVERFLOW_BOUND = 65504.0
EPSILON = 1e-06
MESH = pl.DeviceIdType.MESH
F32 = jnp.float32
BF16 = jnp.bfloat16


def dot(a, b, contract=((1,), (0,))):
    return lax.dot_general(a, b, (contract, ((), ())), preferred_element_type=F32)


def each(first, last, body):
    def step(i, _):
        body(i)
        return 0

    lax.fori_loop(first, last, step, 0)


def wrap(a, n):
    return lax.rem(a, jnp.int32(n))


def over(a, n):
    return lax.div(a, jnp.int32(n))


def remote(source, target, send, recv, device):
    return pltpu.make_async_remote_copy(
        source, target, send, recv, device_id=device, device_id_type=MESH
    )


def kernel(
    exponent_ref, grad_hbm, q_hbm, k_hbm, v_hbm, w_hbm,
    gq_hbm, gk_hbm, gv_hbm, gw_ref, scalars_ref,
    q_ref, k_ref, v_ref, in_sem, gq_ref, gk_ref, gv_ref, out_sem,
    gf, wt, part, hop, xout, xin, att, ctx_t, acc, gc, own_sum, stats,
    g_send, g_recv, sib_send, sib_recv, w_send, w_recv, wx_send, wx_recv,
    r_send, r_recv, x_send, x_recv, s_send, s_recv,
):
    dp = lax.axis_index("dp")
    mp = lax.axis_index("mp")
    xh, z = over(dp, NZ), wrap(dp, NZ)
    y, xl, c = over(mp, 4), wrap(over(mp, 2), 2), wrap(mp, 2)
    factor = HD ** (-0.5)

    near_y = y + 1 - 2 * wrap(y, 2)
    wide_y, opposite_y = wrap(near_y + 2, NY), wrap(y + 2, NY)
    me, peer = y * 2 + xl, y * 2 + 1 - xl
    near, near_peer = near_y * 2 + xl, near_y * 2 + 1 - xl
    wide, wide_peer = wide_y * 2 + xl, wide_y * 2 + 1 - xl
    opposite, opposite_peer = opposite_y * 2 + xl, opposite_y * 2 + 1 - xl

    def to_mp(index):
        return {"dp": dp, "mp": index}

    def to_dp(index):
        return {"dp": index, "mp": mp}

    to_near, to_wide = to_mp(near * 2 + c), to_mp(wide * 2 + c)
    to_peer, to_sibling = to_mp(peer * 2 + c), to_mp(me * 2 + 1 - c)
    right = to_dp(xh * NZ + wrap(z + 1, NZ))
    left = to_dp(xh * NZ + wrap(z + NZ - 1, NZ))
    far = to_dp((1 - xh) * NZ + z)

    barrier = pltpu.get_barrier_semaphore()
    neighbours = (to_near, to_wide, to_peer, to_sibling, right, left, far)
    for device in neighbours:
        pl.semaphore_signal(barrier, inc=1, device_id=device, device_id_type=MESH)
    loads = [
        pltpu.make_async_copy(source, target, in_sem.at[i])
        for i, (source, target) in enumerate((
            (q_hbm, q_ref), (k_hbm, k_ref), (v_hbm, v_ref),
            (grad_hbm, gf.at[mp]), (w_hbm, wt.at[xh, z]),
        ))
    ]
    for load in loads:
        load.start()

    exponent = exponent_ref[0]
    scaling = lax.shift_left(jnp.int32(1), exponent).astype(F32)
    inverse = lax.shift_left(jnp.int32(1), 24 - exponent).astype(F32) * (2.0 ** -24)

    def g_copy(p, h, slot, device):
        piece = gf.at[p * 2 + c, h]
        return remote(piece, piece, g_send.at[slot], g_recv.at[p, h], device)

    def g_own(h, slot, device):
        return remote(
            grad_hbm.at[h], gf.at[mp, h], g_send.at[slot], g_recv.at[me, h], device
        )

    def g_wait(p, h):
        g_copy(p, h, 0, to_peer).wait_recv()

    def sib_copy(p, cc):
        piece = gf.at[p * 2 + cc]
        return remote(piece, piece, sib_send.at[p], sib_recv.at[p], to_sibling)

    def w_copy(step, direction, source=None):
        piece = wt.at[xh, wrap(z + NZ - step if direction == 0 else z + step, NZ)]
        return remote(
            piece if source is None else source, piece,
            w_send.at[direction, step], w_recv.at[direction, step],
            right if direction == 0 else left,
        )

    def w_arrived(step, direction):
        index = wrap(z + NZ - step - 1 if direction == 0 else z + step + 1, NZ)
        piece = wt.at[xh, index]
        remote(
            piece, piece, w_send.at[direction, step], w_recv.at[direction, step],
            right if direction == 0 else left,
        ).wait_recv()

    def w_step(step):
        for direction in range(2):
            if step <= (8, 7)[direction]:
                w_arrived(step - 1, direction)
            if step < (8, 7)[direction]:
                w_copy(step, direction).start()

    def wx_copy(index, half):
        piece = wt.at[half, index]
        return remote(piece, piece, wx_send.at[index], wx_recv.at[index], far)

    def pair_of(order):
        return wrap(over(z, 2) + (0, 1, 7, 2, 6, 3, 5, 4)[order], 8)

    def wx_pair(order):
        for i in range(2):
            wx_copy(2 * pair_of(order) + i, xh).start()

    def add_context(order):
        pair = pair_of(order)
        for i in range(2):
            wx_copy(2 * pair + i, 1 - xh).wait_recv()
        for half in range(2):
            rows = wt[half, pl.ds(2 * pair, 2)].reshape(MINE, HEADS)
            acc[...] += dot(gf[half * 8 + pair].reshape(TOK, MINE), rows)

    def attention_backward(b, h):
        rows, lanes = slice(b * SEQ, (b + 1) * SEQ), slice(h * HD, (h + 1) * HD)
        attention = att[b * 2 + h]
        grad = gc[rows, lanes]
        gv_ref[rows, lanes] = (dot(attention.T.astype(BF16), grad) * inverse).astype(BF16)
        grad_attention = dot(grad, v_ref[rows, lanes], ((1,), (1,)))
        row_dots = jnp.sum(attention * grad_attention, axis=-1, keepdims=True)
        grad_scores = attention * (grad_attention - row_dots) * factor
        gq_ref[rows, lanes] = (
            dot(grad_scores.astype(BF16), k_ref[rows, lanes]) * inverse
        ).astype(BF16)
        gk_ref[rows, lanes] = (
            dot(grad_scores.T.astype(BF16), q_ref[rows, lanes]) * inverse
        ).astype(BF16)

    def partial_of(m):
        block = dot(ctx_t[...], gf[m].reshape(TOK, MINE))
        turned = (block.T * scaling).astype(BF16)
        half, pair = over(m, 8), wrap(m, 8)
        part[half, 2 * pair] = turned[:COLS]
        part[half, 2 * pair + 1] = turned[COLS:]

    def own_partial(p):
        partial_of(p * 2 + c)

    def sib_partial(p):
        sib_copy(p, 1 - c).wait_recv()
        partial_of(p * 2 + 1 - c)

    first = over(y, 2)

    def half_of(turn):
        return first if turn == 0 else 1 - first

    def r_copy(step, direction, turn, piece, source):
        return remote(
            source, hop.at[direction, step, turn, piece],
            r_send.at[direction, step, turn, piece], r_recv.at[direction, step, turn, piece],
            right if direction == 0 else left,
        )

    def r_part(step, direction, turn, piece):
        dest = wrap(z + 8 - step if direction == 0 else z + NZ - 7 + step, NZ)
        return part.at[half_of(turn), dest, piece * CUT : (piece + 1) * CUT]

    def r_start(turn):
        for piece in range(2):
            for direction in range(2):
                r_copy(0, direction, turn, piece, r_part(0, direction, turn, piece)).start()

    def r_arrived(step, direction, turn, piece):
        r_copy(step, direction, turn, piece, hop.at[direction, step, turn, piece]).wait_recv()

    def r_step(step, turn):
        for piece in range(2):
            for direction in range(2):
                if step < (8, 7)[direction]:
                    slot = hop.at[direction, step - 1, turn, piece]
                    r_arrived(step - 1, direction, turn, piece)
                    slot[...] = (
                        slot[...].astype(F32) + r_part(step, direction, turn, piece)[...].astype(F32)
                    ).astype(BF16)
                    r_copy(step, direction, turn, piece, slot).start()

    def total(turn, piece):
        return (
            r_part(8, 0, turn, piece)[...].astype(F32)
            + hop[0, 7, turn, piece].astype(F32) + hop[1, 6, turn, piece].astype(F32)
        )

    def crossing(piece):
        return remote(xout.at[piece], xin.at[piece], x_send.at[piece], x_recv.at[piece], far)

    def finish(turn):
        for piece in range(2):
            r_arrived(7, 0, turn, piece)
            r_arrived(6, 1, turn, piece)

            @pl.when(xh == half_of(turn))
            def _():
                own_sum[piece] = total(turn, piece)

            @pl.when(xh != half_of(turn))
            def _():
                xout[piece] = total(turn, piece).astype(BF16)
                crossing(piece).start()

    pl.semaphore_wait(barrier, len(neighbours))
    own_to_peer = [g_own(0, 0, to_peer), g_own(1, 3, to_peer)]
    own_to_near = [g_own(0, 1, to_near), g_own(1, 4, to_near)]
    own_to_wide = [g_own(0, 2, to_wide), g_own(1, 5, to_wide)]
    peer_to_near, near_to_peer = g_copy(peer, 0, 6, to_near), g_copy(near, 1, 7, to_peer)
    near_to_wide = g_copy(near, 1, 8, to_wide)
    peer_to_wide = [g_copy(peer, 0, 9, to_wide), g_copy(peer, 1, 10, to_wide)]
    wide_to_near, opposite_to_peer = g_copy(wide, 0, 11, to_near), g_copy(opposite, 1, 12, to_peer)
    wide_peer_to_near = g_copy(wide_peer, 0, 13, to_near)

    own_to_near[0].start()
    own_to_peer[0].start()
    own_to_wide[0].start()
    w_copy(0, 0, w_hbm).start()
    w_copy(0, 1, w_hbm).start()
    remote(grad_hbm, gf.at[mp], sib_send.at[me], sib_recv.at[me], to_sibling).start()

    for load in loads:
        load.wait()
    for b in range(2):
        for h in range(2):
            rows, lanes = slice(b * SEQ, (b + 1) * SEQ), slice(h * HD, (h + 1) * HD)
            scores = dot(q_ref[rows, lanes], k_ref[rows, lanes], ((1,), (1,))) * factor
            raised = jnp.exp(scores - jnp.max(scores, axis=-1, keepdims=True))
            attention = raised / jnp.sum(raised, axis=-1, keepdims=True)
            att[b * 2 + h] = attention
            context = dot(attention.astype(BF16), v_ref[rows, lanes])
            ctx_t[lanes, rows] = context.T.astype(BF16)

    for sends in (own_to_near, own_to_peer, own_to_wide):
        sends[0].wait_send()
        sends[1].start()
    w_step(1)
    own_partial(me)
    sib_partial(me)
    w_step(2)
    g_wait(peer, 0)
    own_to_near[1].wait_send()
    peer_to_near.start()
    g_wait(near, 1)
    own_to_peer[1].wait_send()
    near_to_peer.start()
    own_to_wide[1].wait_send()
    near_to_wide.start()
    g_wait(peer, 1)
    sib_copy(peer, c).start()
    g_wait(near, 0)
    sib_copy(near, c).start()
    own_partial(peer)
    own_partial(near)
    g_wait(wide, 0)
    g_wait(wide, 1)
    sib_copy(wide, c).start()
    sib_partial(peer)
    sib_partial(near)
    w_step(3)
    peer_to_near.wait_send()
    wide_to_near.start()
    near_to_wide.wait_send()
    peer_to_wide[0].start()
    g_wait(near_peer, 0)
    g_wait(near_peer, 1)
    sib_copy(near_peer, c).start()
    g_wait(opposite, 1)
    near_to_peer.wait_send()
    opposite_to_peer.start()
    own_partial(near_peer)
    sib_partial(near_peer)
    r_start(0)
    w_step(4)
    own_partial(wide)
    sib_partial(wide)
    wide_to_near.wait_send()
    g_wait(wide_peer, 0)
    wide_peer_to_near.start()
    peer_to_wide[0].wait_send()
    peer_to_wide[1].start()
    g_wait(opposite, 0)
    sib_copy(opposite, c).start()
    wx_pair(0)
    r_step(1, 0)
    own_partial(opposite)
    w_step(5)
    sib_partial(opposite)
    g_wait(wide_peer, 1)
    sib_copy(wide_peer, c).start()
    g_wait(opposite_peer, 1)
    g_wait(opposite_peer, 0)
    sib_copy(opposite_peer, c).start()
    r_step(2, 0)
    own_partial(wide_peer)
    own_partial(opposite_peer)
    sib_partial(wide_peer)
    sib_partial(opposite_peer)
    r_start(1)
    wx_pair(1)
    w_step(6)
    r_step(3, 0)
    r_step(1, 1)
    wx_pair(2)
    w_step(7)
    r_step(4, 0)
    r_step(2, 1)
    w_step(8)
    wx_pair(3)
    wx_pair(4)
    acc[...] = jnp.zeros_like(acc)
    r_step(5, 0)
    r_step(3, 1)
    wx_pair(5)
    wx_pair(6)
    add_context(0)
    r_step(6, 0)
    r_step(4, 1)
    wx_pair(7)
    add_context(1)
    r_step(7, 0)
    r_step(5, 1)
    add_context(2)
    add_context(3)
    finish(0)
    r_step(6, 1)
    for copy in (peer_to_wide[1], opposite_to_peer, wide_peer_to_near):
        copy.wait_send()
    each(0, 8, lambda p: sib_copy(p, c).wait_send())
    add_context(4)
    add_context(5)
    r_step(7, 1)
    for direction in range(2):
        each(0, (8, 7)[direction], lambda step: w_copy(step, direction).wait_send())
    add_context(6)
    finish(1)
    add_context(7)
    gc[...] = (acc[...] * scaling).astype(BF16)
    attention_backward(0, 0)
    attention_backward(0, 1)
    for piece in range(2):
        crossing(piece).wait_recv()
        own_sum[piece] += xin[piece].astype(F32)
    summed = own_sum[...].reshape(COLS, HEADS)
    unscaled = summed * inverse

    def fold(a):
        return a.reshape(COLS // 8, 8, HEADS)

    squares = jnp.sum(fold(unscaled * unscaled), axis=0)
    sizes = jnp.max(fold(jnp.abs(summed)), axis=0)
    stats[0, 0, 0] = squares[:, :128] + squares[:, 128:]
    stats[0, 0, 1] = jnp.maximum(sizes[:, :128], sizes[:, 128:])

    x_core = (xh * 2 + xl) * 2 + c

    def s_targets(turn):
        if turn < 2:
            return [to_dp(xh * NZ + wrap(z + i * 4 ** turn, NZ)) for i in (2, 3, 1)]
        if turn == 2:
            return [to_mp(wrap(y + i, NY) * 4 + xl * 2 + c) for i in (2, 1, 3)]
        found = []
        for i in (4, 5, 3, 2, 6, 1, 7):
            g = wrap(x_core + i, 8)
            found.append({"dp": over(g, 4) * NZ + z, "mp": y * 4 + wrap(g, 4)})
        return found

    def s_copies(turn):
        return [
            remote(
                stats.at[turn, 0], stats.at[turn, i + 1],
                s_send.at[turn, i], s_recv.at[turn, i], device,
            )
            for i, device in enumerate(s_targets(turn))
        ]

    def s_start(turn):
        for copy in s_copies(turn):
            copy.start()

    def s_finish(turn):
        copies = s_copies(turn)
        for copy in copies:
            copy.wait_recv()
        count = len(copies) + 1
        return jnp.sum(stats[turn, :count, 0], axis=0), jnp.max(stats[turn, :count, 1], axis=0)

    s_start(0)

    attention_backward(1, 0)
    stats[1, 0, 0], stats[1, 0, 1] = s_finish(0)
    s_start(1)
    each(0, NZ, lambda i: wx_copy(i, xh).wait_send())
    attention_backward(1, 1)
    stores = [
        pltpu.make_async_copy(source, target, out_sem.at[i])
        for i, (source, target) in enumerate(
            ((gq_ref, gq_hbm), (gk_ref, gk_hbm), (gv_ref, gv_hbm))
        )
    ]
    for store in stores:
        store.start()
    stats[2, 0, 0], stats[2, 0, 1] = s_finish(1)
    s_start(2)
    stats[3, 0, 0], stats[3, 0, 1] = s_finish(2)
    s_start(3)
    for direction in range(2):
        for turn in range(2):
            each(
                0, (8, 7)[direction],
                lambda step: [
                    r_copy(step, direction, turn, piece, part.at[0, 0, :CUT]).wait_send()
                    for piece in range(2)
                ],
            )
    for piece in range(2):
        crossing(piece).wait_send()
    for store in stores:
        store.wait()
    for turn in range(3):
        for copy in s_copies(turn):
            copy.wait_send()
    squares, sizes = s_finish(3)
    squares, largest = jnp.sum(squares, keepdims=True), jnp.max(sizes, keepdims=True)
    grad_magnitude = jnp.sqrt(squares / float(H * HD * D) + EPSILON)
    clipping = jnp.minimum(1.0, 1.0 / grad_magnitude)
    gw_ref[...] = (own_sum[...].reshape(COLS, HEADS) * inverse * clipping).astype(BF16)
    scalars_ref[0] = jnp.broadcast_to(jnp.log2(OVERFLOW_BOUND / (largest + EPSILON)), (8, 128))
    scalars_ref[1] = jnp.broadcast_to(grad_magnitude, (8, 128))
    for copy in s_copies(3):
        copy.wait_send()


def hand_over(
    gq, gk, gv, gw, scalars, gq_out, gk_out, gv_out, gw_out, headroom, magnitude,
    gq_held, gk_held, gv_held, gw_held, in_sem, out_sem,
):
    held = (gq_held, gk_held, gv_held, gw_held)
    loads = [
        pltpu.make_async_copy(source, block, in_sem.at[i])
        for i, (source, block) in enumerate(zip((gq, gk, gv, gw), held))
    ]
    stores = [
        pltpu.make_async_copy(block, target, out_sem.at[i])
        for i, (block, target) in enumerate(zip(held, (gq_out, gk_out, gv_out, gw_out)))
    ]
    for load in loads:
        load.start()
    headroom[0] = jnp.max(scalars[0])
    magnitude[0] = jnp.max(scalars[1])
    for load, store in zip(loads, stores):
        load.wait()
        store.start()
    for store in stores:
        store.wait()


def shards(grad_out, queries, key_rows, value_rows, out_weight, scale_exponent):
    vmem = pl.BlockSpec(memory_space=pltpu.VMEM)
    smem = pl.BlockSpec(memory_space=pltpu.SMEM)
    hbm = pl.BlockSpec(memory_space=pltpu.HBM)
    dma = pltpu.SemaphoreType.DMA
    shape = jax.ShapeDtypeStruct
    results = [shape((TOK, HEADS), BF16)] * 3 + [shape((COLS, HEADS), BF16)]
    outs = pl.pallas_call(
        kernel,
        out_shape=results + [shape((2, 8, 128), F32)],
        in_specs=[smem] + [hbm] * 5,
        out_specs=[hbm] * 3 + [vmem] * 2,
        scratch_shapes=[
            pltpu.VMEM((TOK, HEADS), BF16),
            pltpu.VMEM((TOK, HEADS), BF16),
            pltpu.VMEM((TOK, HEADS), BF16),
            dma((5,)),
            pltpu.VMEM((TOK, HEADS), BF16),
            pltpu.VMEM((TOK, HEADS), BF16),
            pltpu.VMEM((TOK, HEADS), BF16),
            dma((3,)),
            pltpu.VMEM((16, 2, SEQ, MINE), BF16),
            pltpu.VMEM((2, NZ, COLS, HEADS), BF16),
            pltpu.VMEM((2, NZ, COLS, HEADS), BF16),
            pltpu.VMEM((2, 8, 2, 2, CUT, HEADS), BF16),
            pltpu.VMEM((2, CUT, HEADS), BF16),
            pltpu.VMEM((2, CUT, HEADS), BF16),
            pltpu.VMEM((4, SEQ, SEQ), F32),
            pltpu.VMEM((HEADS, TOK), BF16),
            pltpu.VMEM((TOK, HEADS), F32),
            pltpu.VMEM((TOK, HEADS), BF16),
            pltpu.VMEM((2, CUT, HEADS), F32),
            pltpu.VMEM((4, 8, 2, 8, 128), F32),
            dma((14,)), dma((8, 2)), dma((8,)), dma((8,)),
            dma((2, 8)), dma((2, 8)), dma((NZ,)), dma((NZ,)),
            dma((2, 8, 2, 2)), dma((2, 8, 2, 2)), dma((2,)), dma((2,)),
            dma((4, 7)), dma((4, 7)),
        ],
        compiler_params=pltpu.CompilerParams(
            collective_id=0, has_side_effects=True
        ),
    )(
        scale_exponent.reshape(1), grad_out.reshape(2, SEQ, MINE),
        queries, key_rows, value_rows, out_weight.T,
    )
    grad_query, grad_key, grad_value, grad_weight, headroom, magnitude = pl.pallas_call(
        hand_over,
        out_shape=results + [shape((1,), F32)] * 2,
        in_specs=[hbm] * 4 + [vmem],
        out_specs=[hbm] * 4 + [smem] * 2,
        scratch_shapes=[pltpu.VMEM((TOK, HEADS), BF16)] * 3
        + [pltpu.VMEM((COLS, HEADS), BF16), dma((4,)), dma((4,))],
    )(*outs)
    return (
        grad_query, grad_key, grad_value, grad_weight.T,
        headroom.reshape(()), magnitude.reshape(()),
    )


def solution(mesh):
    placed = (P("dp", "mp"), P("dp", "mp"), P("dp", "mp"), P("dp", "mp"), P("mp", "dp"), P())
    return jax.shard_map(
        shards,
        mesh=mesh,
        in_specs=placed,
        out_specs=(P("dp", "mp"), P("dp", "mp"), P("dp", "mp"), P("mp", "dp"), P(), P()),
        check_vma=False,
    )
```
